256 devices in a mesh: pln: 16 (over x, y), wall: 16 (over z, core).
Axes of the slice: x: 4, y: 4, z: 8, core: 2. Of those that a mesh axis runs over, the one named last changes fastest.
Arguments:
- vel_x: float32 [64, 2048, 1024], P('wall', 'pln'), may hold values from -4 to 4
- vel_y: float32 [64, 2048, 1024], P('wall', 'pln'), may hold values from -4 to 4
- vel_z: float32 [64, 2048, 1024], P('wall', 'pln'), may hold values from -4 to 4
- cell_metric: float32 [64], replicated, may hold values from 8 to 64
- face_metric: float32 [65], replicated, may hold values from 16 to 32
Outputs:
- pressure: float32 [2, 64, 512, 2048], P(None, 'wall', 'pln')
The draws below stay inside these ranges and needn't reach their ends.
All inputs are finite; a program needn't handle non-finite values.
Results may differ from the reference program's by a relative error of at most 0.0003.
Values sent between devices are 32-bit elements; how exact they have to be, the bound alone decides.
A program may use at most 128 MiB of HBM per device.

```python
import math
import jax
import jax.numpy as jnp
from jax import lax

NX = 2048
NZ = 1024
NY = 64
NZH = 512


def draw_vel_y(key, part):
    return jax.random.truncated_normal(key, -4.0, 4.0, (NY, NX, NZ), jnp.float32)


def level_of(own_key, dims, cuts, least, largest):
    gain, own = 1.0, jax.random.fold_in(own_key, 6)
    for axis_at, blocks in cuts:
        draws = jnp.exp(jax.random.uniform(jax.random.fold_in(own, axis_at), (blocks,), jnp.float32, least / len(cuts), largest / len(cuts)))
        gain = gain * jnp.repeat(draws, dims[axis_at] // blocks).reshape([-1 if axis == axis_at else 1 for axis in range(len(dims))])
    return gain


def bell_draw(stream_key, extent, deviation, limit, cuts=(), held_as=jnp.bfloat16):
    result = deviation * jax.random.normal(stream_key, extent, jnp.float32)
    if cuts:
        result = result * level_of(stream_key, extent, cuts, -0.22, 0.18)
    return jnp.clip(result, -limit, limit).astype(held_as)


def setup_inputs(seed: int = 0) -> dict:
    streams_of = jax.random.split(jax.random.key(seed), 6)
    vel_x = bell_draw(streams_of[0], (NY, NX, NZ), 1.0, 4.0, ((0, 16), (1, 16)), jnp.float32)
    vel_y = draw_vel_y(jax.random.fold_in(streams_of[5], 71), 0)
    vel_z = bell_draw(streams_of[2], (NY, NX, NZ), 1.0, 4.0, ((0, 16), (1, 16)), jnp.float32)
    cell_metric = jnp.clip(jnp.exp(jax.random.uniform(streams_of[3], (NY,), jnp.float32, math.log(8.0), math.log(64.0))), 8.0, 64.0)
    face_metric = jnp.clip(jnp.exp(jax.random.uniform(streams_of[4], (NY + 1,), jnp.float32, math.log(16.0), math.log(32.0))), 16.0, 32.0)
    return {"vel_x": vel_x, "vel_y": vel_y, "vel_z": vel_z, "cell_metric": cell_metric, "face_metric": face_metric}


def wave_square(kz_first, kz_count, kx_first, kx_count, modes_x, points_z):
    kz_index = (kz_first + jnp.arange(kz_count, dtype=jnp.int32)).astype(jnp.float32)
    kx_index = (kx_first + jnp.arange(kx_count, dtype=jnp.int32)).astype(jnp.float32)
    along_x = 2.0 - 2.0 * jnp.cos((2.0 * math.pi / modes_x) * kx_index)
    along_z = 2.0 - 2.0 * jnp.cos((2.0 * math.pi / points_z) * kz_index)
    return along_z[:, None] + along_x[None, :]


def row_bands(metric_row, low_row, high_row, square):
    lower_band = -metric_row * low_row
    upper_band = -metric_row * high_row
    diag_band = metric_row * (low_row + high_row) + square
    return lower_band, upper_band, diag_band


def sweep_down(rhs_real, rhs_imag, metric, face_low, face_high, square, entering):
    def one_row(carried, inputs):
        ratio_in, real_in, imag_in = carried
        row_real, row_imag, metric_row, low_row, high_row = inputs
        lower_band, upper_band, diag_band = row_bands(metric_row, low_row, high_row, square)
        pivots = diag_band - lower_band * ratio_in
        ratio_out = upper_band / pivots
        real_out = (-row_real - lower_band * real_in) / pivots
        imag_out = (-row_imag - lower_band * imag_in) / pivots
        return (ratio_out, real_out, imag_out), (ratio_out, real_out, imag_out)

    return lax.scan(one_row, entering, (rhs_real, rhs_imag, metric, face_low, face_high))


def sweep_up(ratios, reduced_real, reduced_imag, from_above):
    def one_row(carried, inputs):
        real_next, imag_next = carried
        ratio_row, real_row, imag_row = inputs
        real_here = real_row - ratio_row * real_next
        imag_here = imag_row - ratio_row * imag_next
        return (real_here, imag_here), (real_here, imag_here)

    return lax.scan(one_row, from_above, (ratios, reduced_real, reduced_imag), reverse=True)


def reference(vel_x, vel_y, vel_z, cell_metric, face_metric):
    diverge = (jnp.roll(vel_x, -1, 1) - jnp.roll(vel_x, 1, 1)) * 0.5
    padded = jnp.pad(vel_y, ((1, 1), (0, 0), (0, 0)))
    diverge = diverge + cell_metric[:, None, None] * (padded[2:] - padded[:-2]) * 0.5
    diverge = diverge + (jnp.roll(vel_z, -1, 2) - jnp.roll(vel_z, 1, 2)) * 0.5
    half_spec = jnp.fft.rfft(diverge, axis=2, norm="ortho")[:, :, :NZH]
    spectrum = jnp.fft.fft(half_spec, axis=1, norm="ortho")
    spectrum = jnp.transpose(spectrum, (0, 2, 1))
    real_part = jnp.real(spectrum).astype(jnp.float32)
    imag_part = jnp.imag(spectrum).astype(jnp.float32)
    square = wave_square(0, NZH, 0, NX, NX, NZ)
    zero_plane = jnp.zeros((NZH, NX), jnp.float32)
    unused, (ratios, reduced_real, reduced_imag) = sweep_down(real_part, imag_part, cell_metric, face_metric[:-1], face_metric[1:], square, (zero_plane, zero_plane, zero_plane))
    unused, (press_real, press_imag) = sweep_up(ratios, reduced_real, reduced_imag, (zero_plane, zero_plane))
    return jnp.stack([press_real, press_imag])
```

```python
import functools
import math

import jax
import jax.numpy as jnp
import numpy as np
from jax import lax
from jax.experimental import pallas as pl
from jax.experimental.pallas import tpu as pltpu
from jax.sharding import PartitionSpec as P
import ml_dtypes

MESH = pl.DeviceIdType.MESH
F32 = jnp.float32
BF16 = jnp.bfloat16
NX, NZ, NY = 2048, 1024, 64
PLN, CHIPS, ROWS = 16, 8, 8
PEERS = 2 * PLN
NT = (((1,), (1,)), ((), ()))
NN = (((1,), (0,)), ((), ()))


def halves(table):
    high = table.astype(ml_dtypes.bfloat16)
    low = (table - high.astype(np.float64)).astype(ml_dtypes.bfloat16)
    return np.stack([high, low])


@functools.lru_cache(None)
def tables():
    points = np.arange(512, dtype=np.float64)
    z_parts = []
    for parity in range(2):
        n = 2 * np.arange(256, dtype=np.int64) + parity
        phase = 2.0 * np.pi / NZ * ((n[:, None] * np.arange(512)[None, :]) % NZ)
        pair = np.stack([np.cos(phase), -np.sin(phase)]) / math.sqrt(NZ)
        rows = pair.reshape(2, PEERS, 8, 512).transpose(1, 0, 2, 3).reshape(512, 512)
        z_parts.append(halves(rows))
    z_table = np.stack(z_parts)
    lane = np.arange(128)
    s = 8 * (lane % 16) + lane // 16
    phase = 2.0 * np.pi / 128 * ((lane[:, None] * s[None, :]) % 128)
    cos, sin = -np.cos(phase) / math.sqrt(NX), -np.sin(phase) / math.sqrt(NX)
    x_table = halves(np.block([[cos, -sin], [sin, cos]]))
    turn = 2.0 * np.pi / NX * (np.arange(16)[:, None] * lane[None, :])
    twiddle = np.stack([np.cos(turn), -np.sin(turn)], axis=1).astype(np.float32)
    twiddle = np.broadcast_to(twiddle[:, :, None, :], (16, 2, 8, 128)).copy()
    m = np.arange(NX, dtype=np.float64)
    along_x = (2.0 - 2.0 * np.cos(2.0 * np.pi / NX * m)).astype(np.float32).reshape(16, 1, 128)
    along_x = np.broadcast_to(along_x, (16, 8, 128)).copy()
    n = np.arange(512, dtype=np.float64)
    along_z = (2.0 - 2.0 * np.cos(2.0 * np.pi / NZ * n)).astype(np.float32)
    along_z = along_z.reshape(PEERS, 8, 2).transpose(0, 2, 1)[..., None]
    along_z = np.broadcast_to(along_z, (PEERS, 2, 8, 128)).copy()
    return z_table, x_table, twiddle, along_x, along_z


def times(a, b):
    return a[0] * b[0] - a[1] * b[1], a[0] * b[1] + a[1] * b[0]


def add(a, b):
    return a[0] + b[0], a[1] + b[1]


def sub(a, b):
    return a[0] - b[0], a[1] - b[1]


def minus_i(a):
    return a[1], -a[0]


def four(a):
    s02, d02, s13, d13 = add(a[0], a[2]), sub(a[0], a[2]), add(a[1], a[3]), sub(a[1], a[3])
    d13 = minus_i(d13)
    return [add(s02, s13), add(d02, d13), sub(s02, s13), sub(d02, d13)]


def by_sixteenth(a, k):
    if k == 0:
        return a
    if k == 4:
        return minus_i(a)
    if k == 2:
        h = math.sqrt(0.5)
        return (a[0] + a[1]) * h, (a[1] - a[0]) * h
    if k == 6:
        h = math.sqrt(0.5)
        return (a[1] - a[0]) * h, (a[0] + a[1]) * (-h)
    angle = -2.0 * math.pi * k / 16
    c, s = math.cos(angle), math.sin(angle)
    return a[0] * c - a[1] * s, a[0] * s + a[1] * c


def sixteen(a):
    inner = [four([a[4 * p1 + p2] for p1 in range(4)]) for p2 in range(4)]
    out = [None] * 16
    for t1 in range(4):
        outer = four([by_sixteenth(inner[p2][t1], p2 * t1) for p2 in range(4)])
        for t2 in range(4):
            out[t1 + 4 * t2] = outer[t2]
    return out


def dot3(a_high, a_low, b_high, b_low, dims):
    dot = functools.partial(lax.dot_general, dimension_numbers=dims, preferred_element_type=F32)
    return dot(a_high, b_high) + (dot(a_low, b_high) + dot(a_high, b_low))


def split(value):
    high = value.astype(BF16)
    return high, (value - high.astype(F32)).astype(BF16)


def kernel(
    vel_x, vel_y, vel_z, cell, face, z_table, x_table, twiddle, along_x, along_z,
    out,
    vx, vy, vz, edge_x, dhigh, dlow, ztab, xtab, twid, kx, kz,
    zout, recv, xin, xo, spec, gain, ratio, low_end, high_end,
    chain, zsend, zrecv, zback, zdone, stage,
    in_sem, halo_send, halo_recv, xs_sem, xr_sem, own_sem, zs_sem, zr_sem, bs_sem, br_sem, end_sem, swap_send, swap_recv,
):
    pln, wall = lax.axis_index("pln"), lax.axis_index("wall")
    chip, core = lax.div(wall, 2), lax.rem(wall, 2)
    me = 2 * pln + core

    inputs = [
        pltpu.make_async_copy(vel_x, vx.at[:, pl.ds(8, 128), :], in_sem.at[0]),
        pltpu.make_async_copy(vel_z, vz, in_sem.at[1]),
        pltpu.make_async_copy(vel_y, vy.at[pl.ds(1, 4)], in_sem.at[2]),
        pltpu.make_async_copy(z_table, ztab, in_sem.at[3]),
        pltpu.make_async_copy(x_table, xtab, in_sem.at[4]),
        pltpu.make_async_copy(twiddle, twid, in_sem.at[5]),
        pltpu.make_async_copy(along_x, kx, in_sem.at[6]),
        pltpu.make_async_copy(along_z.at[me], kz, in_sem.at[7]),
    ]
    for copy in inputs:
        copy.start()

    barrier = pltpu.get_barrier_semaphore()

    def greet(pln_to, wall_to):
        pl.semaphore_signal(barrier, inc=1, device_id=(pln_to, wall_to), device_id_type=MESH)

    def peer(step):
        to = lax.rem(me + step, PEERS)
        return to, lax.div(to, 2), 2 * chip + lax.rem(to, 2)

    def greet_peer(step, none):
        to, pln_to, wall_to = peer(step)
        greet(pln_to, wall_to)
        return none

    def greet_chip(step, none):
        greet(pln, 2 * lax.rem(chip + step, CHIPS) + core)
        return none

    lax.fori_loop(1, PEERS, greet_peer, 0)
    lax.fori_loop(1, CHIPS, greet_chip, 0)
    greet(pln, lax.rem(wall + 2 * core + 15, 16))
    pl.semaphore_wait(barrier, PEERS - 1 + CHIPS - 1 + 1)

    def remote(src, dst, send_sem, recv_sem, pln_to, wall_to):
        return pltpu.make_async_remote_copy(
            src_ref=src, dst_ref=dst, send_sem=send_sem, recv_sem=recv_sem,
            device_id=(pln_to, wall_to), device_id_type=MESH,
        )

    after, before = lax.rem(pln + 1, PLN), lax.rem(pln + PLN - 1, PLN)
    above, below = lax.rem(wall + 1, 16), lax.rem(wall + 15, 16)
    halos = [
        remote(vel_y.at[3], vy.at[0], halo_send.at[0], halo_recv.at[0], pln, above),
        remote(vel_y.at[0], vy.at[5], halo_send.at[1], halo_recv.at[1], pln, below),
        remote(vel_x.at[:, pl.ds(127, 1), :], edge_x.at[0], halo_send.at[2], halo_recv.at[2], after, wall),
        remote(vel_x.at[:, pl.ds(0, 1), :], edge_x.at[1], halo_send.at[3], halo_recv.at[3], before, wall),
    ]
    for copy in halos:
        copy.start()
    inputs[0].wait()
    inputs[1].wait()
    inputs[2].wait()
    halos[2].wait()
    halos[3].wait()
    for j in range(4):
        vx[j, 7:8, :] = edge_x[0, j]
        vx[j, 136:137, :] = edge_x[1, j]

    def diverge_row(j):
        metric = cell[4 * wall + j] * 0.5
        from_low = jnp.where((wall == 0) & (j == 0), 0.0, metric)
        from_high = jnp.where((wall == 15) & (j == 3), 0.0, metric)
        for first in range(0, 128, 32):
            rows = slice(first, first + 32)
            along = vx[j, first + 9 : first + 41, :] - vx[j, first + 7 : first + 39, :]
            level = vz[j, rows, :]
            along = along + (pltpu.roll(level, NZ - 1, 1) - pltpu.roll(level, 1, 1))
            total = along * 0.5 + (vy[j + 2, rows, :] * from_high - vy[j, rows, :] * from_low)
            left, right = total[:, :512], total[:, 512:]
            dhigh[0, j, rows, :], dlow[0, j, rows, :] = split(left + right)
            dhigh[1, j, rows, :], dlow[1, j, rows, :] = split(left - right)

    def inner_row(j, none):
        diverge_row(j)
        return none

    lax.fori_loop(1, 3, inner_row, 0)
    halos[0].wait()
    halos[1].wait()

    def outer_row(i, none):
        diverge_row(3 * i)
        return none

    lax.fori_loop(0, 2, outer_row, 0)
    inputs[3].wait()

    def out_copy(k, step):
        to, pln_to, wall_to = peer(step)
        return remote(
            zout.at[k, pl.ds(pl.multiple_of(16 * to, 16), 16), :], recv.at[k, core, pln],
            xs_sem.at[k, step], xr_sem.at[k, step], pln_to, wall_to,
        )

    def in_copy(k, step):
        source = lax.rem(me + PEERS - step, PEERS)
        slot = recv.at[k, lax.rem(source, 2), lax.div(source, 2)]
        return pltpu.make_async_copy(slot, slot, xr_sem.at[k, step])

    def own_copy(k):
        return pltpu.make_async_copy(
            zout.at[k, pl.ds(pl.multiple_of(16 * me, 16), 16), :], recv.at[k, core, pln], own_sem.at[k]
        )

    for k in range(2):
        def z_step(pair, none, k=k):
            rows = pl.ds(2 * pair, 2)
            lanes = pl.ds(pl.multiple_of(256 * pair, 256), 256)
            zout[k, :, lanes] = dot3(
                ztab[k, 0], ztab[k, 1],
                dhigh[k, rows].reshape(256, 512), dlow[k, rows].reshape(256, 512), NT,
            )
            return none

        lax.fori_loop(0, 2, z_step, 0)

        def send_step(step, none, k=k):
            out_copy(k, step).start()
            return none

        lax.fori_loop(1, PEERS, send_step, 0)
        own_copy(k).start()

    for copy in inputs[4:]:
        copy.wait()

    def bands(row, square):
        metric, low, high = cell[row], face[row], face[row + 1]
        return -metric * low, -metric * high, metric * (low + high) + square

    def eliminate(first, square):
        gains, ratios, lowers, entered = [], [], [], []
        for j in range(ROWS):
            lower, upper, diag = bands(first + j, square)
            inverse = 1.0 / (diag if j == 0 else diag - lower * ratios[-1])
            gains.append(inverse)
            ratios.append(upper * inverse)
            entered.append((-lower) * inverse if j == 0 else (-lower) * entered[-1] * inverse)
            lowers.append(lower)
        return gains, ratios, entered

    def matrix_step(at, none):
        k, u = lax.div(at, 16), lax.rem(at, 16)
        gains, ratios, entered = eliminate(8 * chip, kx[u] + kz[k])
        from_low, from_high = entered[7], -ratios[7]
        for j in range(ROWS - 1, -1, -1):
            if j < ROWS - 1:
                from_low = entered[j] - ratios[j] * from_low
                from_high = -ratios[j] * from_high
            gain[k, u, j] = gains[j]
            ratio[k, u, j] = ratios[j]
            low_end[k, u, j] = from_low
            high_end[k, u, j] = from_high
        return none

    lax.fori_loop(0, 32, matrix_step, 0)

    def chain_step(block, held):
        heads = []
        for at in range(4):
            k, i = at // 2, at % 2
            gains, ratios, entered = eliminate(8 * block, kx[2 * chip + i] + kz[k])
            top_low, top_high = entered[7], -ratios[7]
            low, high = top_low, top_high
            for j in range(ROWS - 2, -1, -1):
                low, high = entered[j] - ratios[j] * low, -ratios[j] * high
            head = held[at]
            inverse = 1.0 / (1.0 - low * head)
            chain[k, i, block, 0] = low * inverse
            chain[k, i, block, 1] = high * inverse
            chain[k, i, block, 2] = inverse
            chain[k, i, block, 3] = top_low
            chain[k, i, block, 4] = head
            head = top_high + top_low * head * (high * inverse)
            chain[k, i, block, 5] = head
            heads.append(head)
        return tuple(heads)

    zero = jnp.zeros((8, 128), F32)
    lax.fori_loop(0, CHIPS, chain_step, (zero,) * 4)

    lane = lax.broadcasted_iota(jnp.int32, (8, 128), 1)

    def chip_copy(k, step):
        to = lax.rem(chip + step, CHIPS)
        return remote(
            zsend.at[k, to], zrecv.at[k, chip], zs_sem.at[k, step], zr_sem.at[k, step], pln, 2 * to + core
        )

    def chip_in(k, step, buffer, sems):
        slot = buffer.at[k, lax.rem(chip + CHIPS - step, CHIPS)]
        return pltpu.make_async_copy(slot, slot, sems.at[k, step])

    def back_copy(k, step):
        to = lax.rem(chip + step, CHIPS)
        return remote(
            zback.at[k, to], zdone.at[k, chip], bs_sem.at[k, step], br_sem.at[k, step], pln, 2 * to + core
        )

    def loop(first, last, step):
        def body(at, none):
            step(at)
            return none

        lax.fori_loop(first, last, body, 0)

    def spectrum_part(k):
        loop(1, PEERS, lambda step: in_copy(k, step).wait())
        own_copy(k).wait()

        def points(row):
            side, j = lax.div(row, 4), lax.rem(row, 4)
            lanes = pl.ds(pl.multiple_of(128 * j, 128), 128)
            rows = pl.ds(pl.multiple_of(8 * row, 8), 8)
            held = [(recv[k, side, p, 0:8, lanes], recv[k, side, p, 8:16, lanes]) for p in range(PLN)]
            for t, value in enumerate(sixteen(held)):
                if t:
                    value = times(value, (twid[t, 0], twid[t, 1]))
                xin[t, rows, 0:128] = value[0]
                xin[t, rows, 128:256] = value[1]

        loop(0, ROWS, points)

        def product(group):
            some = pl.ds(4 * group, 4)
            high, low = split(xin[some].reshape(256, 256))
            xo[some] = dot3(high, low, xtab[0], xtab[1], NN).reshape(4, 64, 256)

        loop(0, 4, product)

        def order(row):
            rows = pl.ds(pl.multiple_of(8 * row, 8), 8)
            for c in range(2):
                held = [xo[t, rows, 128 * c : 128 * c + 128] for t in range(16)]
                held = [pltpu.roll(value, t, 1) if t else value for t, value in enumerate(held)]
                for bit in range(4):
                    chosen = (lane & (1 << bit)) != 0
                    held = [jnp.where(chosen, held[(t + (1 << bit)) % 16], held[t]) for t in range(16)]
                for u in range(16):
                    value = held[(16 - u) % 16]
                    spec[k, u, row, c] = pltpu.roll(value, 128 - u, 1) if u else value

        loop(0, ROWS, order)

        def sweep(u):
            to, i = lax.div(u, 2), lax.rem(u, 2)
            for c in range(2):
                reduced = []
                for j in range(ROWS):
                    value = spec[k, u, j, c]
                    if j:
                        lower = -cell[8 * chip + j] * face[8 * chip + j]
                        value = value - lower * reduced[-1]
                    reduced.append(value * gain[k, u, j])
                here = reduced[-1]
                spec[k, u, ROWS - 1, c] = here
                zsend[k, to, i, 2 + c] = here
                for j in range(ROWS - 2, -1, -1):
                    here = reduced[j] - ratio[k, u, j] * here
                    spec[k, u, j, c] = here
                zsend[k, to, i, c] = here

        loop(0, 16, sweep)
        loop(1, CHIPS, lambda step: chip_copy(k, step).start())
        zrecv[k, chip] = zsend[k, chip]

    def chain_part(k):
        loop(1, CHIPS, lambda step: chip_in(k, step, zrecv, zr_sem).wait())
        for i in range(2):
            for c in range(2):
                lead = zero
                ends, heads = [], []
                for block in range(CHIPS):
                    y_low, y_high = zrecv[k, block, i, c], zrecv[k, block, i, 2 + c]
                    end = y_low * chain[k, i, block, 2] + chain[k, i, block, 0] * lead
                    lead = y_high + chain[k, i, block, 3] * (lead + chain[k, i, block, 4] * end)
                    ends.append(end)
                    heads.append(lead)
                from_high = zero
                for block in range(CHIPS - 1, -1, -1):
                    zback[k, block, i, 2 + c] = from_high
                    last = heads[block] + chain[k, i, block, 5] * from_high
                    if block < CHIPS - 1:
                        zback[k, block + 1, i, c] = last
                    from_high = ends[block] + chain[k, i, block, 1] * from_high
                zback[k, 0, i, c] = zero
        loop(1, CHIPS, lambda step: back_copy(k, step).start())
        zdone[k, chip] = zback[k, chip]

    my_rows = pl.ds(pl.multiple_of(16 * core, 16), 16)

    def place(u):
        return out.at[:, :, my_rows, pl.ds(pl.multiple_of(128 * u, 128), 128)]

    def swap_copy(u):
        return remote(
            stage.at[1 - core, u], place(u), swap_send.at[u], swap_recv.at[u], pln, wall + 1 - 2 * core
        )

    def keep_copy(u):
        return pltpu.make_async_copy(stage.at[core, u], place(u), end_sem.at[u])

    def result_part(k):
        loop(1, CHIPS, lambda step: chip_in(k, step, zdone, br_sem).wait())

        def finish(u):
            to, i = lax.div(u, 2), lax.rem(u, 2)
            for c in range(2):
                from_low, from_high = zdone[k, to, i, c], zdone[k, to, i, 2 + c]
                for j in range(ROWS):
                    value = spec[k, u, j, c] + low_end[k, u, j] * from_low + high_end[k, u, j] * from_high
                    stage[j // 4, u, c, j % 4, pl.ds(k, 8, stride=2), :] = value
            if k == 1:
                swap_copy(u).start()
                keep_copy(u).start()

        loop(0, 16, finish)

    spectrum_part(0)
    chain_part(0)
    spectrum_part(1)
    chain_part(1)
    result_part(0)
    result_part(1)

    for k in range(2):
        loop(1, PEERS, lambda step: out_copy(k, step).wait_send())
        loop(1, CHIPS, lambda step: chip_copy(k, step).wait_send())
        loop(1, CHIPS, lambda step: back_copy(k, step).wait_send())
    loop(0, 16, lambda u: keep_copy(u).wait())
    loop(0, 16, lambda u: swap_copy(u).wait())


def per_device(vel_x, vel_y, vel_z, cell_metric, face_metric):
    anywhere = pl.BlockSpec(memory_space=pl.ANY)
    scalars = pl.BlockSpec(memory_space=pltpu.SMEM)
    dma = pltpu.SemaphoreType.DMA
    return pl.pallas_call(
        kernel,
        out_shape=jax.ShapeDtypeStruct((2, 4, 32, NX), F32),
        in_specs=[anywhere] * 3 + [scalars] * 2 + [anywhere] * 5,
        out_specs=anywhere,
        scratch_shapes=[
            pltpu.VMEM((4, 144, NZ), F32),
            pltpu.VMEM((6, 128, NZ), F32),
            pltpu.VMEM((4, 128, NZ), F32),
            pltpu.VMEM((2, 4, 1, NZ), F32),
            pltpu.VMEM((2, 4, 128, 512), BF16),
            pltpu.VMEM((2, 4, 128, 512), BF16),
            pltpu.VMEM((2, 2, 512, 512), BF16),
            pltpu.VMEM((2, 256, 256), BF16),
            pltpu.VMEM((16, 2, 8, 128), F32),
            pltpu.VMEM((16, 8, 128), F32),
            pltpu.VMEM((2, 8, 128), F32),
            pltpu.VMEM((2, 512, 512), F32),
            pltpu.VMEM((2, 2, PLN, 16, 512), F32),
            pltpu.VMEM((16, 64, 256), F32),
            pltpu.VMEM((16, 64, 256), F32),
            pltpu.VMEM((2, 16, ROWS, 2, 8, 128), F32),
            pltpu.VMEM((2, 16, ROWS, 8, 128), F32),
            pltpu.VMEM((2, 16, ROWS, 8, 128), F32),
            pltpu.VMEM((2, 16, ROWS, 8, 128), F32),
            pltpu.VMEM((2, 16, ROWS, 8, 128), F32),
            pltpu.VMEM((2, 2, CHIPS, 6, 8, 128), F32),
            pltpu.VMEM((2, CHIPS, 2, 4, 8, 128), F32),
            pltpu.VMEM((2, CHIPS, 2, 4, 8, 128), F32),
            pltpu.VMEM((2, CHIPS, 2, 4, 8, 128), F32),
            pltpu.VMEM((2, CHIPS, 2, 4, 8, 128), F32),
            pltpu.VMEM((2, 16, 2, 4, 16, 128), F32),
            dma((8,)),
            dma((4,)),
            dma((4,)),
            dma((2, PEERS)),
            dma((2, PEERS)),
            dma((2,)),
            dma((2, CHIPS)),
            dma((2, CHIPS)),
            dma((2, CHIPS)),
            dma((2, CHIPS)),
            dma((16,)),
            dma((16,)),
            dma((16,)),
        ],
        compiler_params=pltpu.CompilerParams(
            collective_id=0, has_side_effects=True, vmem_limit_bytes=48 * 1024 * 1024
        ),
    )(vel_x, vel_y, vel_z, cell_metric, face_metric, *tables())


def solution(mesh):
    in_specs = (P("wall", "pln", None), P("wall", "pln", None), P("wall", "pln", None), P(), P())
    return jax.shard_map(
        per_device, mesh=mesh, in_specs=in_specs, out_specs=P(None, "wall", "pln", None), check_vma=False
    )
```

```python
import functools
import math

import jax
import jax.numpy as jnp
import numpy as np
from jax import lax
from jax.experimental import pallas as pl
from jax.experimental.pallas import tpu as pltpu
from jax.sharding import PartitionSpec as P
import ml_dtypes

MESH = pl.DeviceIdType.MESH
F32 = jnp.float32
BF16 = jnp.bfloat16
NX, NZ, NY = 2048, 1024, 64
PLN, CHIPS, ROWS = 16, 8, 8
PEERS = 2 * PLN
NT = (((1,), (1,)), ((), ()))
NN = (((1,), (0,)), ((), ()))


def halves(table):
    high = table.astype(ml_dtypes.bfloat16)
    low = (table - high.astype(np.float64)).astype(ml_dtypes.bfloat16)
    return np.stack([high, low])


@functools.lru_cache(None)
def tables():
    points = np.arange(512, dtype=np.float64)
    z_parts = []
    for parity in range(2):
        n = 2 * np.arange(256, dtype=np.int64) + parity
        phase = 2.0 * np.pi / NZ * ((n[:, None] * np.arange(512)[None, :]) % NZ)
        pair = np.stack([np.cos(phase), -np.sin(phase)]) / math.sqrt(NZ)
        rows = pair.reshape(2, PEERS, 8, 512).transpose(1, 0, 2, 3).reshape(512, 512)
        z_parts.append(halves(rows))
    z_table = np.stack(z_parts)
    lane = np.arange(128)
    s = 8 * (lane % 16) + lane // 16
    phase = 2.0 * np.pi / 128 * ((lane[:, None] * s[None, :]) % 128)
    cos, sin = -np.cos(phase) / math.sqrt(NX), -np.sin(phase) / math.sqrt(NX)
    x_table = halves(np.block([[cos, -sin], [sin, cos]]))
    turn = 2.0 * np.pi / NX * (np.arange(16)[:, None] * lane[None, :])
    twiddle = np.stack([np.cos(turn), -np.sin(turn)], axis=1).astype(np.float32)
    twiddle = np.broadcast_to(twiddle[:, :, None, :], (16, 2, 8, 128)).copy()
    m = np.arange(NX, dtype=np.float64)
    along_x = (2.0 - 2.0 * np.cos(2.0 * np.pi / NX * m)).astype(np.float32).reshape(16, 1, 128)
    along_x = np.broadcast_to(along_x, (16, 8, 128)).copy()
    n = np.arange(512, dtype=np.float64)
    along_z = (2.0 - 2.0 * np.cos(2.0 * np.pi / NZ * n)).astype(np.float32)
    along_z = along_z.reshape(PEERS, 8, 2).transpose(0, 2, 1)[..., None]
    along_z = np.broadcast_to(along_z, (PEERS, 2, 8, 128)).copy()
    return z_table, x_table, twiddle, along_x, along_z


def times(a, b):
    return a[0] * b[0] - a[1] * b[1], a[0] * b[1] + a[1] * b[0]


def add(a, b):
    return a[0] + b[0], a[1] + b[1]


def sub(a, b):
    return a[0] - b[0], a[1] - b[1]


def minus_i(a):
    return a[1], -a[0]


def four(a):
    s02, d02, s13, d13 = add(a[0], a[2]), sub(a[0], a[2]), add(a[1], a[3]), sub(a[1], a[3])
    d13 = minus_i(d13)
    return [add(s02, s13), add(d02, d13), sub(s02, s13), sub(d02, d13)]


def by_sixteenth(a, k):
    if k == 0:
        return a
    if k == 4:
        return minus_i(a)
    if k == 2:
        h = math.sqrt(0.5)
        return (a[0] + a[1]) * h, (a[1] - a[0]) * h
    if k == 6:
        h = math.sqrt(0.5)
        return (a[1] - a[0]) * h, (a[0] + a[1]) * (-h)
    angle = -2.0 * math.pi * k / 16
    c, s = math.cos(angle), math.sin(angle)
    return a[0] * c - a[1] * s, a[0] * s + a[1] * c


def sixteen(a):
    inner = [four([a[4 * p1 + p2] for p1 in range(4)]) for p2 in range(4)]
    out = [None] * 16
    for t1 in range(4):
        outer = four([by_sixteenth(inner[p2][t1], p2 * t1) for p2 in range(4)])
        for t2 in range(4):
            out[t1 + 4 * t2] = outer[t2]
    return out


def dot3(a_high, a_low, b_high, b_low, dims):
    dot = functools.partial(lax.dot_general, dimension_numbers=dims, preferred_element_type=F32)
    return dot(a_high, b_high) + (dot(a_low, b_high) + dot(a_high, b_low))


def split(value):
    high = value.astype(BF16)
    return high, (value - high.astype(F32)).astype(BF16)


def kernel(
    vel_x, vel_y, vel_z, cell_metric, face_metric, z_table, x_table, twiddle, along_x, along_z,
    out,
    cell, face, vx, vy, vz, edge_x, dhigh, dlow, ztab, xtab, twid, kx, kz,
    zout, recv, xin, xo, spec, gain, ratio, low_end, high_end,
    chain, zsend, zrecv, zback, zdone, stage,
    in_sem, halo_send, halo_recv, xs_sem, xr_sem, own_sem, zs_sem, zr_sem, bs_sem, br_sem, end_sem, swap_send, swap_recv,
):
    pln, wall = lax.axis_index("pln"), lax.axis_index("wall")
    chip, core = lax.div(wall, 2), lax.rem(wall, 2)
    me = 2 * pln + core

    inputs = [
        pltpu.make_async_copy(vel_x, vx.at[:, pl.ds(8, 128), :], in_sem.at[0]),
        pltpu.make_async_copy(vel_z, vz, in_sem.at[1]),
        pltpu.make_async_copy(vel_y, vy.at[pl.ds(1, 4)], in_sem.at[2]),
        pltpu.make_async_copy(z_table, ztab, in_sem.at[3]),
        pltpu.make_async_copy(x_table, xtab, in_sem.at[4]),
        pltpu.make_async_copy(twiddle, twid, in_sem.at[5]),
        pltpu.make_async_copy(along_x, kx, in_sem.at[6]),
        pltpu.make_async_copy(along_z.at[me], kz, in_sem.at[7]),
        pltpu.make_async_copy(cell_metric, cell, in_sem.at[8]),
        pltpu.make_async_copy(face_metric, face, in_sem.at[9]),
    ]
    for copy in inputs:
        copy.start()

    barrier = pltpu.get_barrier_semaphore()

    def greet(pln_to, wall_to):
        pl.semaphore_signal(barrier, inc=1, device_id=(pln_to, wall_to), device_id_type=MESH)

    def peer(step):
        to = lax.rem(me + step, PEERS)
        return to, lax.div(to, 2), 2 * chip + lax.rem(to, 2)

    def greet_peer(step, none):
        to, pln_to, wall_to = peer(step)
        greet(pln_to, wall_to)
        return none

    def greet_chip(step, none):
        greet(pln, 2 * lax.rem(chip + step, CHIPS) + core)
        return none

    lax.fori_loop(1, PEERS, greet_peer, 0)
    lax.fori_loop(1, CHIPS, greet_chip, 0)
    greet(pln, lax.rem(wall + 2 * core + 15, 16))
    pl.semaphore_wait(barrier, PEERS - 1 + CHIPS - 1 + 1)

    def remote(src, dst, send_sem, recv_sem, pln_to, wall_to):
        return pltpu.make_async_remote_copy(
            src_ref=src, dst_ref=dst, send_sem=send_sem, recv_sem=recv_sem,
            device_id=(pln_to, wall_to), device_id_type=MESH,
        )

    after, before = lax.rem(pln + 1, PLN), lax.rem(pln + PLN - 1, PLN)
    above, below = lax.rem(wall + 1, 16), lax.rem(wall + 15, 16)
    halos = [
        remote(vel_x.at[:, pl.ds(127, 1), :], edge_x.at[0], halo_send.at[0], halo_recv.at[0], after, wall),
        remote(vel_x.at[:, pl.ds(0, 1), :], edge_x.at[1], halo_send.at[1], halo_recv.at[1], before, wall),
        remote(vel_y.at[3], vy.at[0], halo_send.at[2], halo_recv.at[2], pln, above),
        remote(vel_y.at[0], vy.at[5], halo_send.at[3], halo_recv.at[3], pln, below),
    ]
    for copy in halos:
        copy.start()
    for copy in inputs[:3] + inputs[8:]:
        copy.wait()
    halos[0].wait()
    halos[1].wait()
    for j in range(4):
        vx[j, 7:8, :] = edge_x[0, j]
        vx[j, 136:137, :] = edge_x[1, j]

    def diverge_row(j, slot):
        metric = cell[4 * wall + j] * 0.5
        from_low = jnp.where((wall == 0) & (j == 0), 0.0, metric)
        from_high = jnp.where((wall == 15) & (j == 3), 0.0, metric)
        for first in range(0, 128, 32):
            rows = slice(first, first + 32)
            along = vx[j, first + 9 : first + 41, :] - vx[j, first + 7 : first + 39, :]
            level = vz[j, rows, :]
            along = along + (pltpu.roll(level, NZ - 1, 1) - pltpu.roll(level, 1, 1))
            total = along * 0.5 + (vy[j + 2, rows, :] * from_high - vy[j, rows, :] * from_low)
            left, right = total[:, :512], total[:, 512:]
            dhigh[0, slot, rows, :], dlow[0, slot, rows, :] = split(left + right)
            dhigh[1, slot, rows, :], dlow[1, slot, rows, :] = split(left - right)

    def out_copy(k, part, step):
        to, pln_to, wall_to = peer(step)
        return remote(
            zout.at[k, part, pl.ds(pl.multiple_of(16 * to, 16), 16), :], recv.at[k, part, core, pln],
            xs_sem.at[k, part, step], xr_sem.at[k, part, step], pln_to, wall_to,
        )

    def in_copy(k, part, step):
        source = lax.rem(me + PEERS - step, PEERS)
        slot = recv.at[k, part, lax.rem(source, 2), lax.div(source, 2)]
        return pltpu.make_async_copy(slot, slot, xr_sem.at[k, part, step])

    def own_copy(k, part):
        return pltpu.make_async_copy(
            zout.at[k, part, pl.ds(pl.multiple_of(16 * me, 16), 16), :], recv.at[k, part, core, pln],
            own_sem.at[k, part],
        )

    def loop(first, last, step):
        def body(at, none):
            step(at)
            return none

        lax.fori_loop(first, last, body, 0)

    def z_part(k, part):
        slots = slice(2 * part, 2 * part + 2)
        zout[k, part] = dot3(
            ztab[k, 0], ztab[k, 1], dhigh[k, slots].reshape(256, 512), dlow[k, slots].reshape(256, 512), NT
        )

    def send_part(k, part):
        loop(1, PEERS, lambda step: out_copy(k, part, step).start())
        own_copy(k, part).start()

    def sent_part(k, part):
        loop(1, PEERS, lambda step: out_copy(k, part, step).wait_send())

    loop(0, 2, lambda i: diverge_row(1 + i, i))
    inputs[3].wait()
    z_part(0, 0)
    send_part(0, 0)
    z_part(1, 0)
    halos[2].wait()
    halos[3].wait()
    loop(0, 2, lambda i: diverge_row(3 * i, 2 + i))
    z_part(0, 1)
    send_part(0, 1)
    z_part(1, 1)
    sent_part(0, 0)
    send_part(1, 0)
    for copy in inputs[4:8]:
        copy.wait()

    def bands(row, square):
        metric, low, high = cell[row], face[row], face[row + 1]
        return -metric * low, -metric * high, metric * (low + high) + square

    def eliminate(first, square):
        gains, ratios, lowers, entered = [], [], [], []
        for j in range(ROWS):
            lower, upper, diag = bands(first + j, square)
            inverse = 1.0 / (diag if j == 0 else diag - lower * ratios[-1])
            gains.append(inverse)
            ratios.append(upper * inverse)
            entered.append((-lower) * inverse if j == 0 else (-lower) * entered[-1] * inverse)
            lowers.append(lower)
        return gains, ratios, entered

    def matrix_step(at, none):
        k, u = lax.div(at, 16), lax.rem(at, 16)
        gains, ratios, entered = eliminate(8 * chip, kx[u] + kz[k])
        from_low, from_high = entered[7], -ratios[7]
        for j in range(ROWS - 1, -1, -1):
            if j < ROWS - 1:
                from_low = entered[j] - ratios[j] * from_low
                from_high = -ratios[j] * from_high
            gain[k, u, j] = gains[j]
            ratio[k, u, j] = ratios[j]
            low_end[k, u, j] = from_low
            high_end[k, u, j] = from_high
        return none

    lax.fori_loop(0, 32, matrix_step, 0)

    def chain_step(block, held):
        heads = []
        for at in range(4):
            k, i = at // 2, at % 2
            gains, ratios, entered = eliminate(8 * block, kx[2 * chip + i] + kz[k])
            top_low, top_high = entered[7], -ratios[7]
            low, high = top_low, top_high
            for j in range(ROWS - 2, -1, -1):
                low, high = entered[j] - ratios[j] * low, -ratios[j] * high
            head = held[at]
            inverse = 1.0 / (1.0 - low * head)
            chain[k, i, block, 0] = low * inverse
            chain[k, i, block, 1] = high * inverse
            chain[k, i, block, 2] = inverse
            chain[k, i, block, 3] = top_low
            chain[k, i, block, 4] = head
            head = top_high + top_low * head * (high * inverse)
            chain[k, i, block, 5] = head
            heads.append(head)
        return tuple(heads)

    zero = jnp.zeros((8, 128), F32)
    lax.fori_loop(0, CHIPS, chain_step, (zero,) * 4)
    sent_part(0, 1)
    send_part(1, 1)

    lane = lax.broadcasted_iota(jnp.int32, (8, 128), 1)

    def chip_copy(k, step):
        to = lax.rem(chip + step, CHIPS)
        return remote(
            zsend.at[k, to], zrecv.at[k, chip], zs_sem.at[k, step], zr_sem.at[k, step], pln, 2 * to + core
        )

    def chip_in(k, step, buffer, sems):
        slot = buffer.at[k, lax.rem(chip + CHIPS - step, CHIPS)]
        return pltpu.make_async_copy(slot, slot, sems.at[k, step])

    def back_copy(k, step):
        to = lax.rem(chip + step, CHIPS)
        return remote(
            zback.at[k, to], zdone.at[k, chip], bs_sem.at[k, step], br_sem.at[k, step], pln, 2 * to + core
        )

    def spectrum_part(k):
        for part in range(2):
            loop(1, PEERS, lambda step: in_copy(k, part, step).wait())
            own_copy(k, part).wait()

        def points(at):
            side, part, i = lax.div(at, 4), lax.rem(lax.div(at, 2), 2), lax.rem(at, 2)
            row = 4 * side + 1 + i - part + 2 * part * i
            lanes = pl.ds(pl.multiple_of(128 * i, 128), 128)
            rows = pl.ds(pl.multiple_of(8 * row, 8), 8)
            held = [
                (recv[k, part, side, p, 0:8, lanes], recv[k, part, side, p, 8:16, lanes]) for p in range(PLN)
            ]
            for t, value in enumerate(sixteen(held)):
                if t:
                    value = times(value, (twid[t, 0], twid[t, 1]))
                xin[t, rows, 0:128] = value[0]
                xin[t, rows, 128:256] = value[1]

        loop(0, ROWS, points)

        def product(group):
            some = pl.ds(4 * group, 4)
            high, low = split(xin[some].reshape(256, 256))
            xo[some] = dot3(high, low, xtab[0], xtab[1], NN).reshape(4, 64, 256)

        loop(0, 4, product)

        def order(row):
            rows = pl.ds(pl.multiple_of(8 * row, 8), 8)
            for c in range(2):
                held = [xo[t, rows, 128 * c : 128 * c + 128] for t in range(16)]
                held = [pltpu.roll(value, t, 1) if t else value for t, value in enumerate(held)]
                for bit in range(4):
                    chosen = (lane & (1 << bit)) != 0
                    held = [jnp.where(chosen, held[(t + (1 << bit)) % 16], held[t]) for t in range(16)]
                for u in range(16):
                    value = held[(16 - u) % 16]
                    spec[k, u, row, c] = pltpu.roll(value, 128 - u, 1) if u else value

        loop(0, ROWS, order)

        def sweep(u):
            to, i = lax.div(u, 2), lax.rem(u, 2)
            for c in range(2):
                reduced = []
                for j in range(ROWS):
                    value = spec[k, u, j, c]
                    if j:
                        lower = -cell[8 * chip + j] * face[8 * chip + j]
                        value = value - lower * reduced[-1]
                    reduced.append(value * gain[k, u, j])
                here = reduced[-1]
                spec[k, u, ROWS - 1, c] = here
                zsend[k, to, i, 2 + c] = here
                for j in range(ROWS - 2, -1, -1):
                    here = reduced[j] - ratio[k, u, j] * here
                    spec[k, u, j, c] = here
                zsend[k, to, i, c] = here

        loop(0, 16, sweep)
        loop(1, CHIPS, lambda step: chip_copy(k, step).start())
        zrecv[k, chip] = zsend[k, chip]

    def chain_part(k):
        loop(1, CHIPS, lambda step: chip_in(k, step, zrecv, zr_sem).wait())
        for i in range(2):
            for c in range(2):
                lead = zero
                ends, heads = [], []
                for block in range(CHIPS):
                    y_low, y_high = zrecv[k, block, i, c], zrecv[k, block, i, 2 + c]
                    end = y_low * chain[k, i, block, 2] + chain[k, i, block, 0] * lead
                    lead = y_high + chain[k, i, block, 3] * (lead + chain[k, i, block, 4] * end)
                    ends.append(end)
                    heads.append(lead)
                from_high = zero
                for block in range(CHIPS - 1, -1, -1):
                    zback[k, block, i, 2 + c] = from_high
                    last = heads[block] + chain[k, i, block, 5] * from_high
                    if block < CHIPS - 1:
                        zback[k, block + 1, i, c] = last
                    from_high = ends[block] + chain[k, i, block, 1] * from_high
                zback[k, 0, i, c] = zero
        loop(1, CHIPS, lambda step: back_copy(k, step).start())
        zdone[k, chip] = zback[k, chip]

    my_rows = pl.ds(pl.multiple_of(16 * core, 16), 16)

    def place(u):
        return out.at[:, :, my_rows, pl.ds(pl.multiple_of(128 * u, 128), 128)]

    def swap_copy(u):
        return remote(
            stage.at[1 - core, u], place(u), swap_send.at[u], swap_recv.at[u], pln, wall + 1 - 2 * core
        )

    def keep_copy(u):
        return pltpu.make_async_copy(stage.at[core, u], place(u), end_sem.at[u])

    def result_part(k):
        loop(1, CHIPS, lambda step: chip_in(k, step, zdone, br_sem).wait())

        def finish(u):
            to, i = lax.div(u, 2), lax.rem(u, 2)
            for c in range(2):
                from_low, from_high = zdone[k, to, i, c], zdone[k, to, i, 2 + c]
                for j in range(ROWS):
                    value = spec[k, u, j, c] + low_end[k, u, j] * from_low + high_end[k, u, j] * from_high
                    stage[j // 4, u, c, j % 4, pl.ds(k, 8, stride=2), :] = value
            if k == 1:
                swap_copy(u).start()
                keep_copy(u).start()

        loop(0, 16, finish)

    spectrum_part(0)
    chain_part(0)
    spectrum_part(1)
    result_part(0)
    chain_part(1)
    result_part(1)

    sent_part(1, 0)
    sent_part(1, 1)
    for k in range(2):
        loop(1, CHIPS, lambda step: chip_copy(k, step).wait_send())
        loop(1, CHIPS, lambda step: back_copy(k, step).wait_send())
    loop(0, 16, lambda u: keep_copy(u).wait())
    loop(0, 16, lambda u: swap_copy(u).wait())


def per_device(vel_x, vel_y, vel_z, cell_metric, face_metric):
    anywhere = pl.BlockSpec(memory_space=pl.ANY)
    far = pl.BlockSpec(memory_space=pltpu.HBM)
    dma = pltpu.SemaphoreType.DMA
    return pl.pallas_call(
        kernel,
        out_shape=jax.ShapeDtypeStruct((2, 4, 32, NX), F32),
        in_specs=[far] * 10,
        out_specs=anywhere,
        scratch_shapes=[
            pltpu.SMEM((NY,), F32),
            pltpu.SMEM((NY + 1,), F32),
            pltpu.VMEM((4, 144, NZ), F32),
            pltpu.VMEM((6, 128, NZ), F32),
            pltpu.VMEM((4, 128, NZ), F32),
            pltpu.VMEM((2, 4, 1, NZ), F32),
            pltpu.VMEM((2, 4, 128, 512), BF16),
            pltpu.VMEM((2, 4, 128, 512), BF16),
            pltpu.VMEM((2, 2, 512, 512), BF16),
            pltpu.VMEM((2, 256, 256), BF16),
            pltpu.VMEM((16, 2, 8, 128), F32),
            pltpu.VMEM((16, 8, 128), F32),
            pltpu.VMEM((2, 8, 128), F32),
            pltpu.VMEM((2, 2, 512, 256), F32),
            pltpu.VMEM((2, 2, 2, PLN, 16, 256), F32),
            pltpu.VMEM((16, 64, 256), F32),
            pltpu.VMEM((16, 64, 256), F32),
            pltpu.VMEM((2, 16, ROWS, 2, 8, 128), F32),
            pltpu.VMEM((2, 16, ROWS, 8, 128), F32),
            pltpu.VMEM((2, 16, ROWS, 8, 128), F32),
            pltpu.VMEM((2, 16, ROWS, 8, 128), F32),
            pltpu.VMEM((2, 16, ROWS, 8, 128), F32),
            pltpu.VMEM((2, 2, CHIPS, 6, 8, 128), F32),
            pltpu.VMEM((2, CHIPS, 2, 4, 8, 128), F32),
            pltpu.VMEM((2, CHIPS, 2, 4, 8, 128), F32),
            pltpu.VMEM((2, CHIPS, 2, 4, 8, 128), F32),
            pltpu.VMEM((2, CHIPS, 2, 4, 8, 128), F32),
            pltpu.VMEM((2, 16, 2, 4, 16, 128), F32),
            dma((10,)),
            dma((4,)),
            dma((4,)),
            dma((2, 2, PEERS)),
            dma((2, 2, PEERS)),
            dma((2, 2)),
            dma((2, CHIPS)),
            dma((2, CHIPS)),
            dma((2, CHIPS)),
            dma((2, CHIPS)),
            dma((16,)),
            dma((16,)),
            dma((16,)),
        ],
        compiler_params=pltpu.CompilerParams(
            collective_id=0, has_side_effects=True, vmem_limit_bytes=60 * 1024 * 1024
        ),
    )(vel_x, vel_y, vel_z, cell_metric, face_metric, *tables())


def solution(mesh):
    in_specs = (P("wall", "pln", None), P("wall", "pln", None), P("wall", "pln", None), P(), P())
    return jax.shard_map(
        per_device, mesh=mesh, in_specs=in_specs, out_specs=P(None, "wall", "pln", None), check_vma=False
    )
```

```python
import functools
import math

import jax
import jax.numpy as jnp
import numpy as np
from jax import lax
from jax.experimental import pallas as pl
from jax.experimental.pallas import tpu as pltpu
from jax.sharding import PartitionSpec as P
import ml_dtypes

MESH = pl.DeviceIdType.MESH
F32 = jnp.float32
BF16 = jnp.bfloat16
NX, NZ, NY = 2048, 1024, 64
PLN, CHIPS, ROWS = 16, 8, 8
PEERS = 2 * PLN
NT = (((1,), (1,)), ((), ()))
NN = (((1,), (0,)), ((), ()))


def halves(table):
    high = table.astype(ml_dtypes.bfloat16)
    low = (table - high.astype(np.float64)).astype(ml_dtypes.bfloat16)
    return np.stack([high, low])


@functools.lru_cache(None)
def tables():
    points = np.arange(512, dtype=np.float64)
    z_parts = []
    for parity in range(2):
        n = 2 * np.arange(256, dtype=np.int64) + parity
        phase = 2.0 * np.pi / NZ * ((n[:, None] * np.arange(512)[None, :]) % NZ)
        pair = np.stack([np.cos(phase), -np.sin(phase)]) / math.sqrt(NZ)
        rows = pair.reshape(2, PEERS, 8, 512).transpose(1, 0, 2, 3).reshape(512, 512)
        z_parts.append(halves(rows))
    z_table = np.stack(z_parts)
    lane = np.arange(128)
    s = 8 * (lane % 16) + lane // 16
    phase = 2.0 * np.pi / 128 * ((lane[:, None] * s[None, :]) % 128)
    cos, sin = -np.cos(phase) / math.sqrt(NX), -np.sin(phase) / math.sqrt(NX)
    x_table = halves(np.block([[cos, -sin], [sin, cos]]))
    turn = 2.0 * np.pi / NX * (np.arange(16)[:, None] * lane[None, :])
    twiddle = np.stack([np.cos(turn), -np.sin(turn)], axis=1).astype(np.float32)
    twiddle = np.broadcast_to(twiddle[:, :, None, :], (16, 2, 8, 128)).copy()
    m = np.arange(NX, dtype=np.float64)
    along_x = (2.0 - 2.0 * np.cos(2.0 * np.pi / NX * m)).astype(np.float32).reshape(16, 1, 128)
    along_x = np.broadcast_to(along_x, (16, 8, 128)).copy()
    n = np.arange(512, dtype=np.float64)
    along_z = (2.0 - 2.0 * np.cos(2.0 * np.pi / NZ * n)).astype(np.float32)
    along_z = along_z.reshape(PEERS, 8, 2).transpose(0, 2, 1)[..., None]
    along_z = np.broadcast_to(along_z, (PEERS, 2, 8, 128)).copy()
    return z_table, x_table, twiddle, along_x, along_z


def times(a, b):
    return a[0] * b[0] - a[1] * b[1], a[0] * b[1] + a[1] * b[0]


def add(a, b):
    return a[0] + b[0], a[1] + b[1]


def sub(a, b):
    return a[0] - b[0], a[1] - b[1]


def minus_i(a):
    return a[1], -a[0]


def four(a):
    s02, d02, s13, d13 = add(a[0], a[2]), sub(a[0], a[2]), add(a[1], a[3]), sub(a[1], a[3])
    d13 = minus_i(d13)
    return [add(s02, s13), add(d02, d13), sub(s02, s13), sub(d02, d13)]


def by_sixteenth(a, k):
    if k == 0:
        return a
    if k == 4:
        return minus_i(a)
    if k == 2:
        h = math.sqrt(0.5)
        return (a[0] + a[1]) * h, (a[1] - a[0]) * h
    if k == 6:
        h = math.sqrt(0.5)
        return (a[1] - a[0]) * h, (a[0] + a[1]) * (-h)
    angle = -2.0 * math.pi * k / 16
    c, s = math.cos(angle), math.sin(angle)
    return a[0] * c - a[1] * s, a[0] * s + a[1] * c


def sixteen(a):
    inner = [four([a[4 * p1 + p2] for p1 in range(4)]) for p2 in range(4)]
    out = [None] * 16
    for t1 in range(4):
        outer = four([by_sixteenth(inner[p2][t1], p2 * t1) for p2 in range(4)])
        for t2 in range(4):
            out[t1 + 4 * t2] = outer[t2]
    return out


def dot3(a_high, a_low, b_high, b_low, dims):
    dot = functools.partial(lax.dot_general, dimension_numbers=dims, preferred_element_type=F32)
    return dot(a_high, b_high) + (dot(a_low, b_high) + dot(a_high, b_low))


def split(value):
    high = value.astype(BF16)
    return high, (value - high.astype(F32)).astype(BF16)


def kernel(
    vel_x, vel_y, vel_z, cell_metric, face_metric, z_table, x_table, twiddle, along_x, along_z,
    out,
    cell, face, vx, vy, vz, edge_x, dhigh, dlow, ztab, xtab, twid, kx, kz,
    zout, recv, xin, xo, spec, gain, ratio, low_end, high_end,
    chain, zsend, zrecv, zback, zdone, stage,
    in_sem, halo_send, halo_recv, xs_sem, xr_sem, own_sem, zs_sem, zr_sem, bs_sem, br_sem, end_sem, swap_send, swap_recv,
):
    pln, wall = lax.axis_index("pln"), lax.axis_index("wall")
    chip, core = lax.div(wall, 2), lax.rem(wall, 2)
    me = 2 * pln + core

    def x_rows(first, rows):
        return vel_x.at[pl.ds(first, rows)], vx.at[pl.ds(first, rows), pl.ds(8, 128), :]

    def z_rows(first, rows):
        return vel_z.at[pl.ds(first, rows)], vz.at[pl.ds(first, rows)]

    pairs = [
        (vel_y, vy.at[pl.ds(1, 4)]), x_rows(1, 2), z_rows(1, 2), (cell_metric, cell), (z_table, ztab),
        x_rows(0, 1), x_rows(3, 1), z_rows(0, 1), z_rows(3, 1), (face_metric, face),
        (x_table, xtab), (twiddle, twid), (along_x, kx), (along_z.at[me], kz),
    ]
    inputs = [pltpu.make_async_copy(src, dst, in_sem.at[at]) for at, (src, dst) in enumerate(pairs)]
    for copy in inputs:
        copy.start()

    barrier = pltpu.get_barrier_semaphore()

    def greet(pln_to, wall_to):
        pl.semaphore_signal(barrier, inc=1, device_id=(pln_to, wall_to), device_id_type=MESH)

    def peer(step):
        to = lax.rem(me + step, PEERS)
        return to, lax.div(to, 2), 2 * chip + lax.rem(to, 2)

    def greet_peer(step, none):
        to, pln_to, wall_to = peer(step)
        greet(pln_to, wall_to)
        return none

    def greet_chip(step, none):
        greet(pln, 2 * lax.rem(chip + step, CHIPS) + core)
        return none

    lax.fori_loop(1, PEERS, greet_peer, 0)
    lax.fori_loop(1, CHIPS, greet_chip, 0)
    greet(pln, lax.rem(wall + 2 * core + 15, 16))
    pl.semaphore_wait(barrier, PEERS - 1 + CHIPS - 1 + 1)

    def remote(src, dst, send_sem, recv_sem, pln_to, wall_to):
        return pltpu.make_async_remote_copy(
            src_ref=src, dst_ref=dst, send_sem=send_sem, recv_sem=recv_sem,
            device_id=(pln_to, wall_to), device_id_type=MESH,
        )

    after, before = lax.rem(pln + 1, PLN), lax.rem(pln + PLN - 1, PLN)
    above, below = lax.rem(wall + 1, 16), lax.rem(wall + 15, 16)
    halos = [
        remote(vel_x.at[:, pl.ds(127, 1), :], edge_x.at[0], halo_send.at[0], halo_recv.at[0], after, wall),
        remote(vel_x.at[:, pl.ds(0, 1), :], edge_x.at[1], halo_send.at[1], halo_recv.at[1], before, wall),
        remote(vel_y.at[3], vy.at[0], halo_send.at[2], halo_recv.at[2], pln, above),
        remote(vel_y.at[0], vy.at[5], halo_send.at[3], halo_recv.at[3], pln, below),
    ]
    for copy in halos:
        copy.start()
    def diverge_row(j, slot, firsts):
        metric = cell[4 * wall + j] * 0.5
        from_low = jnp.where((wall == 0) & (j == 0), 0.0, metric)
        from_high = jnp.where((wall == 15) & (j == 3), 0.0, metric)
        for first in firsts:
            rows = slice(first, first + 32)
            along = vx[j, first + 9 : first + 41, :] - vx[j, first + 7 : first + 39, :]
            level = vz[j, rows, :]
            along = along + (pltpu.roll(level, NZ - 1, 1) - pltpu.roll(level, 1, 1))
            total = along * 0.5 + (vy[j + 2, rows, :] * from_high - vy[j, rows, :] * from_low)
            left, right = total[:, :512], total[:, 512:]
            dhigh[0, slot, rows, :], dlow[0, slot, rows, :] = split(left + right)
            dhigh[1, slot, rows, :], dlow[1, slot, rows, :] = split(left - right)

    def out_copy(k, part, step):
        to, pln_to, wall_to = peer(step)
        return remote(
            zout.at[k, part, pl.ds(pl.multiple_of(16 * to, 16), 16), :], recv.at[k, part, core, pln],
            xs_sem.at[k, part, step], xr_sem.at[k, part, step], pln_to, wall_to,
        )

    def in_copy(k, part, step):
        source = lax.rem(me + PEERS - step, PEERS)
        slot = recv.at[k, part, lax.rem(source, 2), lax.div(source, 2)]
        return pltpu.make_async_copy(slot, slot, xr_sem.at[k, part, step])

    def own_copy(k, part):
        return pltpu.make_async_copy(
            zout.at[k, part, pl.ds(pl.multiple_of(16 * me, 16), 16), :], recv.at[k, part, core, pln],
            own_sem.at[k, part],
        )

    def loop(first, last, step):
        def body(at, none):
            step(at)
            return none

        lax.fori_loop(first, last, body, 0)

    def z_part(k, part):
        slots = slice(2 * part, 2 * part + 2)
        zout[k, part] = dot3(
            ztab[k, 0], ztab[k, 1], dhigh[k, slots].reshape(256, 512), dlow[k, slots].reshape(256, 512), NT
        )

    def send_part(k, part):
        loop(1, PEERS, lambda step: out_copy(k, part, step).start())
        own_copy(k, part).start()

    def sent_part(k, part):
        loop(1, PEERS, lambda step: out_copy(k, part, step).wait_send())

    for copy in inputs[:4]:
        copy.wait()
    loop(0, 2, lambda i: diverge_row(1 + i, i, (32, 64)))
    halos[0].wait()
    halos[1].wait()
    for j in range(4):
        vx[j, 7:8, :] = edge_x[0, j]
        vx[j, 136:137, :] = edge_x[1, j]
    loop(0, 2, lambda i: diverge_row(1 + i, i, (0, 96)))
    inputs[4].wait()
    z_part(0, 0)
    send_part(0, 0)
    z_part(1, 0)
    for copy in inputs[5:10]:
        copy.wait()
    halos[2].wait()
    halos[3].wait()
    loop(0, 2, lambda i: diverge_row(3 * i, 2 + i, (0, 32, 64, 96)))
    z_part(0, 1)
    send_part(0, 1)
    z_part(1, 1)
    sent_part(0, 0)
    send_part(1, 0)
    for copy in inputs[10:]:
        copy.wait()

    def bands(row, square):
        metric, low, high = cell[row], face[row], face[row + 1]
        return -metric * low, -metric * high, metric * (low + high) + square

    def eliminate(first, square):
        gains, ratios, lowers, entered = [], [], [], []
        for j in range(ROWS):
            lower, upper, diag = bands(first + j, square)
            inverse = 1.0 / (diag if j == 0 else diag - lower * ratios[-1])
            gains.append(inverse)
            ratios.append(upper * inverse)
            entered.append((-lower) * inverse if j == 0 else (-lower) * entered[-1] * inverse)
            lowers.append(lower)
        return gains, ratios, entered

    def matrix_step(at, none):
        k, u = lax.div(at, 16), lax.rem(at, 16)
        gains, ratios, entered = eliminate(8 * chip, kx[u] + kz[k])
        from_low, from_high = entered[7], -ratios[7]
        for j in range(ROWS - 1, -1, -1):
            if j < ROWS - 1:
                from_low = entered[j] - ratios[j] * from_low
                from_high = -ratios[j] * from_high
            gain[k, u, j] = gains[j]
            ratio[k, u, j] = ratios[j]
            low_end[k, u, j] = from_low
            high_end[k, u, j] = from_high
        return none

    lax.fori_loop(0, 32, matrix_step, 0)

    def chain_step(block, held):
        heads = []
        for at in range(4):
            k, i = at // 2, at % 2
            gains, ratios, entered = eliminate(8 * block, kx[2 * chip + i] + kz[k])
            top_low, top_high = entered[7], -ratios[7]
            low, high = top_low, top_high
            for j in range(ROWS - 2, -1, -1):
                low, high = entered[j] - ratios[j] * low, -ratios[j] * high
            head = held[at]
            inverse = 1.0 / (1.0 - low * head)
            chain[k, i, block, 0] = low * inverse
            chain[k, i, block, 1] = high * inverse
            chain[k, i, block, 2] = inverse
            chain[k, i, block, 3] = top_low
            chain[k, i, block, 4] = head
            head = top_high + top_low * head * (high * inverse)
            chain[k, i, block, 5] = head
            heads.append(head)
        return tuple(heads)

    zero = jnp.zeros((8, 128), F32)
    lax.fori_loop(0, CHIPS, chain_step, (zero,) * 4)
    sent_part(0, 1)
    send_part(1, 1)

    lane = lax.broadcasted_iota(jnp.int32, (8, 128), 1)

    def chip_copy(k, i, step):
        to = lax.rem(chip + step, CHIPS)
        return remote(
            zsend.at[k, to, i], zrecv.at[k, chip, i], zs_sem.at[k, i, step], zr_sem.at[k, i, step], pln, 2 * to + core
        )

    def chip_in(k, i, step, buffer, sems):
        slot = buffer.at[k, lax.rem(chip + CHIPS - step, CHIPS), i]
        return pltpu.make_async_copy(slot, slot, sems.at[k, i, step])

    def back_copy(k, i, step):
        to = lax.rem(chip + step, CHIPS)
        return remote(
            zback.at[k, to, i], zdone.at[k, chip, i], bs_sem.at[k, i, step], br_sem.at[k, i, step], pln, 2 * to + core
        )

    def spectrum_part(k):
        for part in range(2):
            loop(1, PEERS, lambda step: in_copy(k, part, step).wait())
            own_copy(k, part).wait()

        def points(at):
            side, part, i = lax.div(at, 4), lax.rem(lax.div(at, 2), 2), lax.rem(at, 2)
            row = 4 * side + 1 + i - part + 2 * part * i
            lanes = pl.ds(pl.multiple_of(128 * i, 128), 128)
            rows = pl.ds(pl.multiple_of(8 * row, 8), 8)
            held = [
                (recv[k, part, side, p, 0:8, lanes], recv[k, part, side, p, 8:16, lanes]) for p in range(PLN)
            ]
            for t, value in enumerate(sixteen(held)):
                if t:
                    value = times(value, (twid[t, 0], twid[t, 1]))
                xin[t, rows, 0:128] = value[0]
                xin[t, rows, 128:256] = value[1]

        loop(0, ROWS, points)

        def product(group):
            some = pl.ds(4 * group, 4)
            high, low = split(xin[some].reshape(256, 256))
            xo[some] = dot3(high, low, xtab[0], xtab[1], NN).reshape(4, 64, 256)

        loop(0, 4, product)

        def order(row):
            rows = pl.ds(pl.multiple_of(8 * row, 8), 8)
            for c in range(2):
                held = [xo[t, rows, 128 * c : 128 * c + 128] for t in range(16)]
                held = [pltpu.roll(value, t, 1) if t else value for t, value in enumerate(held)]
                for bit in range(4):
                    chosen = (lane & (1 << bit)) != 0
                    held = [jnp.where(chosen, held[(t + (1 << bit)) % 16], held[t]) for t in range(16)]
                for u in range(16):
                    value = held[(16 - u) % 16]
                    spec[k, u, row, c] = pltpu.roll(value, 128 - u, 1) if u else value

        loop(0, ROWS, order)

        def sweep(to, i):
            u = 2 * to + i
            for c in range(2):
                reduced = []
                for j in range(ROWS):
                    value = spec[k, u, j, c]
                    if j:
                        lower = -cell[8 * chip + j] * face[8 * chip + j]
                        value = value - lower * reduced[-1]
                    reduced.append(value * gain[k, u, j])
                here = reduced[-1]
                spec[k, u, ROWS - 1, c] = here
                zsend[k, to, i, 2 + c] = here
                for j in range(ROWS - 2, -1, -1):
                    here = reduced[j] - ratio[k, u, j] * here
                    spec[k, u, j, c] = here
                zsend[k, to, i, c] = here

        for i in range(2):
            loop(0, CHIPS, lambda to: sweep(to, i))
            loop(1, CHIPS, lambda step: chip_copy(k, i, step).start())
            zrecv[k, chip, i] = zsend[k, chip, i]

    def chain_part(k, i):
        loop(1, CHIPS, lambda step: chip_in(k, i, step, zrecv, zr_sem).wait())
        for c in range(2):
            lead = zero
            ends, heads = [], []
            for block in range(CHIPS):
                y_low, y_high = zrecv[k, block, i, c], zrecv[k, block, i, 2 + c]
                end = y_low * chain[k, i, block, 2] + chain[k, i, block, 0] * lead
                lead = y_high + chain[k, i, block, 3] * (lead + chain[k, i, block, 4] * end)
                ends.append(end)
                heads.append(lead)
            from_high = zero
            for block in range(CHIPS - 1, -1, -1):
                zback[k, block, i, 2 + c] = from_high
                last = heads[block] + chain[k, i, block, 5] * from_high
                if block < CHIPS - 1:
                    zback[k, block + 1, i, c] = last
                from_high = ends[block] + chain[k, i, block, 1] * from_high
            zback[k, 0, i, c] = zero
        loop(1, CHIPS, lambda step: back_copy(k, i, step).start())
        zdone[k, chip, i] = zback[k, chip, i]

    my_rows = pl.ds(pl.multiple_of(16 * core, 16), 16)

    def place(u):
        return out.at[:, :, my_rows, pl.ds(pl.multiple_of(128 * u, 128), 128)]

    def swap_copy(u):
        return remote(
            stage.at[1 - core, u], place(u), swap_send.at[u], swap_recv.at[u], pln, wall + 1 - 2 * core
        )

    def keep_copy(u):
        return pltpu.make_async_copy(stage.at[core, u], place(u), end_sem.at[u])

    def result_part(k, i):
        loop(1, CHIPS, lambda step: chip_in(k, i, step, zdone, br_sem).wait())

        def finish(to):
            u = 2 * to + i
            for c in range(2):
                from_low, from_high = zdone[k, to, i, c], zdone[k, to, i, 2 + c]
                for j in range(ROWS):
                    value = spec[k, u, j, c] + low_end[k, u, j] * from_low + high_end[k, u, j] * from_high
                    stage[j // 4, u, c, j % 4, pl.ds(k, 8, stride=2), :] = value
            if k == 1:
                swap_copy(u).start()
                keep_copy(u).start()

        loop(0, CHIPS, finish)

    spectrum_part(0)
    chain_part(0, 0)
    chain_part(0, 1)
    spectrum_part(1)
    result_part(0, 0)
    result_part(0, 1)
    chain_part(1, 0)
    chain_part(1, 1)
    result_part(1, 0)
    result_part(1, 1)

    sent_part(1, 0)
    sent_part(1, 1)
    for k in range(2):
        for i in range(2):
            loop(1, CHIPS, lambda step: chip_copy(k, i, step).wait_send())
            loop(1, CHIPS, lambda step: back_copy(k, i, step).wait_send())
    loop(0, 16, lambda u: keep_copy(u).wait())
    loop(0, 16, lambda u: swap_copy(u).wait())


def per_device(vel_x, vel_y, vel_z, cell_metric, face_metric):
    anywhere = pl.BlockSpec(memory_space=pl.ANY)
    far = pl.BlockSpec(memory_space=pltpu.HBM)
    dma = pltpu.SemaphoreType.DMA
    return pl.pallas_call(
        kernel,
        out_shape=jax.ShapeDtypeStruct((2, 4, 32, NX), F32),
        in_specs=[far] * 10,
        out_specs=anywhere,
        scratch_shapes=[
            pltpu.SMEM((NY,), F32),
            pltpu.SMEM((NY + 1,), F32),
            pltpu.VMEM((4, 144, NZ), F32),
            pltpu.VMEM((6, 128, NZ), F32),
            pltpu.VMEM((4, 128, NZ), F32),
            pltpu.VMEM((2, 4, 1, NZ), F32),
            pltpu.VMEM((2, 4, 128, 512), BF16),
            pltpu.VMEM((2, 4, 128, 512), BF16),
            pltpu.VMEM((2, 2, 512, 512), BF16),
            pltpu.VMEM((2, 256, 256), BF16),
            pltpu.VMEM((16, 2, 8, 128), F32),
            pltpu.VMEM((16, 8, 128), F32),
            pltpu.VMEM((2, 8, 128), F32),
            pltpu.VMEM((2, 2, 512, 256), F32),
            pltpu.VMEM((2, 2, 2, PLN, 16, 256), F32),
            pltpu.VMEM((16, 64, 256), F32),
            pltpu.VMEM((16, 64, 256), F32),
            pltpu.VMEM((2, 16, ROWS, 2, 8, 128), F32),
            pltpu.VMEM((2, 16, ROWS, 8, 128), F32),
            pltpu.VMEM((2, 16, ROWS, 8, 128), F32),
            pltpu.VMEM((2, 16, ROWS, 8, 128), F32),
            pltpu.VMEM((2, 16, ROWS, 8, 128), F32),
            pltpu.VMEM((2, 2, CHIPS, 6, 8, 128), F32),
            pltpu.VMEM((2, CHIPS, 2, 4, 8, 128), F32),
            pltpu.VMEM((2, CHIPS, 2, 4, 8, 128), F32),
            pltpu.VMEM((2, CHIPS, 2, 4, 8, 128), F32),
            pltpu.VMEM((2, CHIPS, 2, 4, 8, 128), F32),
            pltpu.VMEM((2, 16, 2, 4, 16, 128), F32),
            dma((14,)),
            dma((4,)),
            dma((4,)),
            dma((2, 2, PEERS)),
            dma((2, 2, PEERS)),
            dma((2, 2)),
            dma((2, 2, CHIPS)),
            dma((2, 2, CHIPS)),
            dma((2, 2, CHIPS)),
            dma((2, 2, CHIPS)),
            dma((16,)),
            dma((16,)),
            dma((16,)),
        ],
        compiler_params=pltpu.CompilerParams(
            collective_id=0, has_side_effects=True, vmem_limit_bytes=60 * 1024 * 1024
        ),
    )(vel_x, vel_y, vel_z, cell_metric, face_metric, *tables())


def solution(mesh):
    in_specs = (P("wall", "pln", None), P("wall", "pln", None), P("wall", "pln", None), P(), P())
    return jax.shard_map(
        per_device, mesh=mesh, in_specs=in_specs, out_specs=P(None, "wall", "pln", None), check_vma=False
    )
```

```python
import functools
import math

import jax
import jax.numpy as jnp
import numpy as np
from jax import lax
from jax.experimental import pallas as pl
from jax.experimental.pallas import tpu as pltpu
from jax.sharding import PartitionSpec as P
import ml_dtypes

MESH = pl.DeviceIdType.MESH
F32 = jnp.float32
BF16 = jnp.bfloat16
NX, NZ, NY = 2048, 1024, 64
PLN, CHIPS, ROWS = 16, 8, 8
PEERS = 2 * PLN
NT = (((1,), (1,)), ((), ()))
NN = (((1,), (0,)), ((), ()))


def halves(table):
    high = table.astype(ml_dtypes.bfloat16)
    low = (table - high.astype(np.float64)).astype(ml_dtypes.bfloat16)
    return np.stack([high, low])


@functools.lru_cache(None)
def tables():
    points = np.arange(512, dtype=np.float64)
    z_parts = []
    for parity in range(2):
        n = 2 * np.arange(256, dtype=np.int64) + parity
        phase = 2.0 * np.pi / NZ * ((n[:, None] * np.arange(512)[None, :]) % NZ)
        pair = np.stack([np.cos(phase), -np.sin(phase)]) / math.sqrt(NZ)
        rows = pair.reshape(2, PEERS, 8, 512).transpose(1, 0, 2, 3).reshape(512, 512)
        z_parts.append(halves(rows))
    z_table = np.stack(z_parts)
    lane = np.arange(128)
    s = 8 * (lane % 16) + lane // 16
    phase = 2.0 * np.pi / 128 * ((lane[:, None] * s[None, :]) % 128)
    cos, sin = -np.cos(phase) / math.sqrt(NX), -np.sin(phase) / math.sqrt(NX)
    x_table = halves(np.block([[cos, -sin], [sin, cos]]))
    turn = 2.0 * np.pi / NX * (np.arange(16)[:, None] * lane[None, :])
    twiddle = np.stack([np.cos(turn), -np.sin(turn)], axis=1).astype(np.float32)
    twiddle = np.broadcast_to(twiddle[:, :, None, :], (16, 2, 8, 128)).copy()
    m = np.arange(NX, dtype=np.float64)
    along_x = (2.0 - 2.0 * np.cos(2.0 * np.pi / NX * m)).astype(np.float32).reshape(16, 1, 128)
    along_x = np.broadcast_to(along_x, (16, 8, 128)).copy()
    n = np.arange(512, dtype=np.float64)
    along_z = (2.0 - 2.0 * np.cos(2.0 * np.pi / NZ * n)).astype(np.float32)
    along_z = along_z.reshape(PEERS, 8, 2).transpose(0, 2, 1)[..., None]
    along_z = np.broadcast_to(along_z, (PEERS, 2, 8, 128)).copy()
    return z_table, x_table, twiddle, along_x, along_z


def times(a, b):
    return a[0] * b[0] - a[1] * b[1], a[0] * b[1] + a[1] * b[0]


def add(a, b):
    return a[0] + b[0], a[1] + b[1]


def sub(a, b):
    return a[0] - b[0], a[1] - b[1]


def minus_i(a):
    return a[1], -a[0]


def four(a):
    s02, d02, s13, d13 = add(a[0], a[2]), sub(a[0], a[2]), add(a[1], a[3]), sub(a[1], a[3])
    d13 = minus_i(d13)
    return [add(s02, s13), add(d02, d13), sub(s02, s13), sub(d02, d13)]


def by_sixteenth(a, k):
    if k == 0:
        return a
    if k == 4:
        return minus_i(a)
    if k == 2:
        h = math.sqrt(0.5)
        return (a[0] + a[1]) * h, (a[1] - a[0]) * h
    if k == 6:
        h = math.sqrt(0.5)
        return (a[1] - a[0]) * h, (a[0] + a[1]) * (-h)
    angle = -2.0 * math.pi * k / 16
    c, s = math.cos(angle), math.sin(angle)
    return a[0] * c - a[1] * s, a[0] * s + a[1] * c


def sixteen(a):
    inner = [four([a[4 * p1 + p2] for p1 in range(4)]) for p2 in range(4)]
    out = [None] * 16
    for t1 in range(4):
        outer = four([by_sixteenth(inner[p2][t1], p2 * t1) for p2 in range(4)])
        for t2 in range(4):
            out[t1 + 4 * t2] = outer[t2]
    return out


def dot3(a_high, a_low, b_high, b_low, dims):
    dot = functools.partial(lax.dot_general, dimension_numbers=dims, preferred_element_type=F32)
    return dot(a_high, b_high) + (dot(a_low, b_high) + dot(a_high, b_low))


def split(value):
    high = value.astype(BF16)
    return high, (value - high.astype(F32)).astype(BF16)


def kernel(
    vel_x, vel_y, vel_z, cell_metric, face_metric, z_table, x_table, twiddle, along_x, along_z,
    out,
    cell, face, vx, vy, vz, edge_x, dhigh, dlow, ztab, xtab, twid, kx, kz,
    zout, recv, xin, xo, spec, gain, ratio, low_end, high_end,
    chain, zsend, zrecv, zback, zdone, stage,
    in_sem, halo_send, halo_recv, xs_sem, xr_sem, zs_sem, zr_sem, bs_sem, br_sem, end_sem, swap_send, swap_recv,
):
    pln, wall = lax.axis_index("pln"), lax.axis_index("wall")
    chip, core = lax.div(wall, 2), lax.rem(wall, 2)
    me = 2 * pln + core

    def x_rows(first, rows):
        return vel_x.at[pl.ds(first, rows)], vx.at[pl.ds(first, rows), pl.ds(8, 128), :]

    def z_rows(first, rows):
        return vel_z.at[pl.ds(first, rows)], vz.at[pl.ds(first, rows)]

    pairs = [
        (vel_y, vy.at[pl.ds(1, 4)]), x_rows(1, 2), z_rows(1, 2), (cell_metric, cell), (z_table, ztab),
        x_rows(0, 1), x_rows(3, 1), z_rows(0, 1), z_rows(3, 1), (face_metric, face),
        (x_table, xtab), (twiddle, twid), (along_x, kx), (along_z.at[me], kz),
    ]
    inputs = [pltpu.make_async_copy(src, dst, in_sem.at[at]) for at, (src, dst) in enumerate(pairs)]
    for copy in inputs:
        copy.start()

    barrier = pltpu.get_barrier_semaphore()

    def greet(pln_to, wall_to):
        pl.semaphore_signal(barrier, inc=1, device_id=(pln_to, wall_to), device_id_type=MESH)

    def peer(step):
        to = (me + step) & (PEERS - 1)
        return to, to >> 1, 2 * chip + (to & 1)

    def greet_peer(step, none):
        to, pln_to, wall_to = peer(step)
        greet(pln_to, wall_to)
        return none

    def greet_chip(step, none):
        greet(pln, 2 * lax.rem(chip + step, CHIPS) + core)
        return none

    lax.fori_loop(1, PEERS, greet_peer, 0)
    lax.fori_loop(1, CHIPS, greet_chip, 0)
    greet(pln, lax.rem(wall + 2 * core + 15, 16))
    pl.semaphore_wait(barrier, PEERS - 1 + CHIPS - 1 + 1)

    def remote(src, dst, send_sem, recv_sem, pln_to, wall_to):
        return pltpu.make_async_remote_copy(
            src_ref=src, dst_ref=dst, send_sem=send_sem, recv_sem=recv_sem,
            device_id=(pln_to, wall_to), device_id_type=MESH,
        )

    after, before = lax.rem(pln + 1, PLN), lax.rem(pln + PLN - 1, PLN)
    above, below = lax.rem(wall + 1, 16), lax.rem(wall + 15, 16)
    halos = [
        remote(vel_x.at[:, pl.ds(127, 1), :], edge_x.at[0], halo_send.at[0], halo_recv.at[0], after, wall),
        remote(vel_x.at[:, pl.ds(0, 1), :], edge_x.at[1], halo_send.at[1], halo_recv.at[1], before, wall),
        remote(vel_y.at[3], vy.at[0], halo_send.at[2], halo_recv.at[2], pln, above),
        remote(vel_y.at[0], vy.at[5], halo_send.at[3], halo_recv.at[3], pln, below),
    ]
    for copy in halos:
        copy.start()
    def diverge_row(j, slot, firsts):
        metric = cell[4 * wall + j] * 0.5
        from_low = jnp.where((wall == 0) & (j == 0), 0.0, metric)
        from_high = jnp.where((wall == 15) & (j == 3), 0.0, metric)
        for first in firsts:
            rows = slice(first, first + 32)
            along = vx[j, first + 9 : first + 41, :] - vx[j, first + 7 : first + 39, :]
            level = vz[j, rows, :]
            along = along + (pltpu.roll(level, NZ - 1, 1) - pltpu.roll(level, 1, 1))
            total = along * 0.5 + (vy[j + 2, rows, :] * from_high - vy[j, rows, :] * from_low)
            left, right = total[:, :512], total[:, 512:]
            dhigh[0, slot, rows, :], dlow[0, slot, rows, :] = split(left + right)
            dhigh[1, slot, rows, :], dlow[1, slot, rows, :] = split(left - right)

    def out_copy(k, part, step):
        to, pln_to, wall_to = peer(step)
        return remote(
            zout.at[k, part, pl.ds(pl.multiple_of(16 * to, 16), 16), :], recv.at[k, part, core, pln],
            xs_sem.at[k, part], xr_sem.at[k, part], pln_to, wall_to,
        )

    def arrived_part(k, part):
        pltpu.make_async_copy(recv.at[k, part], recv.at[k, part], xr_sem.at[k, part]).wait()

    def own_copy(k, part):
        return pltpu.make_async_copy(
            zout.at[k, part, pl.ds(pl.multiple_of(16 * me, 16), 16), :], recv.at[k, part, core, pln],
            xr_sem.at[k, part],
        )

    def loop(first, last, step):
        def body(at, none):
            step(at)
            return none

        lax.fori_loop(first, last, body, 0)

    def z_part(k, part):
        slots = slice(2 * part, 2 * part + 2)
        zout[k, part] = dot3(
            ztab[k, 0], ztab[k, 1], dhigh[k, slots].reshape(256, 512), dlow[k, slots].reshape(256, 512), NT
        )

    def send_part(k, part):
        loop(1, PEERS, lambda step: out_copy(k, part, step).start())
        own_copy(k, part).start()

    def sent_part(k, part):
        gone = zout.at[k, part, pl.ds(0, 16 * (PEERS - 1)), :]
        pltpu.make_async_copy(gone, gone, xs_sem.at[k, part]).wait()

    for copy in inputs[:4]:
        copy.wait()
    loop(0, 2, lambda i: diverge_row(1 + i, i, (32, 64)))
    halos[0].wait()
    halos[1].wait()
    for j in range(4):
        vx[j, 7:8, :] = edge_x[0, j]
        vx[j, 136:137, :] = edge_x[1, j]
    loop(0, 2, lambda i: diverge_row(1 + i, i, (0, 96)))
    inputs[4].wait()
    z_part(0, 0)
    send_part(0, 0)
    z_part(1, 0)
    for copy in inputs[5:10]:
        copy.wait()
    halos[2].wait()
    halos[3].wait()
    loop(0, 2, lambda i: diverge_row(3 * i, 2 + i, (0, 32, 64, 96)))
    z_part(0, 1)
    send_part(0, 1)
    z_part(1, 1)
    sent_part(0, 0)
    send_part(1, 0)
    for copy in inputs[10:]:
        copy.wait()

    def bands(row, square):
        metric, low, high = cell[row], face[row], face[row + 1]
        return -metric * low, -metric * high, metric * (low + high) + square

    def eliminate(first, square):
        gains, ratios, lowers, entered = [], [], [], []
        for j in range(ROWS):
            lower, upper, diag = bands(first + j, square)
            inverse = 1.0 / (diag if j == 0 else diag - lower * ratios[-1])
            gains.append(inverse)
            ratios.append(upper * inverse)
            entered.append((-lower) * inverse if j == 0 else (-lower) * entered[-1] * inverse)
            lowers.append(lower)
        return gains, ratios, entered

    def matrix_step(at, none):
        k, u = lax.div(at, 16), lax.rem(at, 16)
        gains, ratios, entered = eliminate(8 * chip, kx[u] + kz[k])
        from_low, from_high = entered[7], -ratios[7]
        for j in range(ROWS - 1, -1, -1):
            if j < ROWS - 1:
                from_low = entered[j] - ratios[j] * from_low
                from_high = -ratios[j] * from_high
            gain[k, u, j] = gains[j]
            ratio[k, u, j] = ratios[j]
            low_end[k, u, j] = from_low
            high_end[k, u, j] = from_high
        return none

    lax.fori_loop(0, 32, matrix_step, 0)

    def chain_step(block, held):
        heads = []
        for at in range(4):
            k, i = at // 2, at % 2
            gains, ratios, entered = eliminate(8 * block, kx[2 * chip + i] + kz[k])
            top_low, top_high = entered[7], -ratios[7]
            low, high = top_low, top_high
            for j in range(ROWS - 2, -1, -1):
                low, high = entered[j] - ratios[j] * low, -ratios[j] * high
            head = held[at]
            inverse = 1.0 / (1.0 - low * head)
            chain[k, i, block, 0] = low * inverse
            chain[k, i, block, 1] = high * inverse
            chain[k, i, block, 2] = inverse
            chain[k, i, block, 3] = top_low
            chain[k, i, block, 4] = head
            head = top_high + top_low * head * (high * inverse)
            chain[k, i, block, 5] = head
            heads.append(head)
        return tuple(heads)

    zero = jnp.zeros((8, 128), F32)
    lax.fori_loop(0, CHIPS, chain_step, (zero,) * 4)
    sent_part(0, 1)
    send_part(1, 1)

    lane = lax.broadcasted_iota(jnp.int32, (8, 128), 1)

    def chip_copy(k, i, step):
        to = lax.rem(chip + step, CHIPS)
        return remote(
            zsend.at[k, to, i], zrecv.at[k, chip, i], zs_sem.at[k, i, step], zr_sem.at[k, i, step], pln, 2 * to + core
        )

    def chip_in(k, i, step, buffer, sems):
        slot = buffer.at[k, lax.rem(chip + CHIPS - step, CHIPS), i]
        return pltpu.make_async_copy(slot, slot, sems.at[k, i, step])

    def back_copy(k, i, step):
        to = lax.rem(chip + step, CHIPS)
        return remote(
            zback.at[k, to, i], zdone.at[k, chip, i], bs_sem.at[k, i, step], br_sem.at[k, i, step], pln, 2 * to + core
        )

    def spectrum_part(k):
        def points(at, part):
            side, i = at >> 1, at & 1
            row = 4 * side + 1 + i - part + 2 * part * i
            lanes = pl.ds(pl.multiple_of(128 * i, 128), 128)
            rows = pl.ds(pl.multiple_of(8 * row, 8), 8)
            held = [
                (recv[k, part, side, p, 0:8, lanes], recv[k, part, side, p, 8:16, lanes]) for p in range(PLN)
            ]
            for t, value in enumerate(sixteen(held)):
                if t:
                    value = times(value, (twid[t, 0], twid[t, 1]))
                xin[t, rows, 0:128] = value[0]
                xin[t, rows, 128:256] = value[1]

        for part in range(2):
            arrived_part(k, part)
            loop(0, 4, lambda at: points(at, part))

        def product(group):
            some = pl.ds(4 * group, 4)
            high, low = split(xin[some].reshape(256, 256))
            xo[some] = dot3(high, low, xtab[0], xtab[1], NN).reshape(4, 64, 256)

        loop(0, 4, product)

        def order(row):
            rows = pl.ds(pl.multiple_of(8 * row, 8), 8)
            for c in range(2):
                held = [xo[t, rows, 128 * c : 128 * c + 128] for t in range(16)]
                held = [pltpu.roll(value, t, 1) if t else value for t, value in enumerate(held)]
                for bit in range(4):
                    chosen = (lane & (1 << bit)) != 0
                    held = [jnp.where(chosen, held[(t + (1 << bit)) % 16], held[t]) for t in range(16)]
                for u in range(16):
                    value = held[(16 - u) % 16]
                    spec[k, u, row, c] = pltpu.roll(value, 128 - u, 1) if u else value

        loop(0, ROWS, order)

        def sweep(to, i):
            u = 2 * to + i
            for c in range(2):
                reduced = []
                for j in range(ROWS):
                    value = spec[k, u, j, c]
                    if j:
                        lower = -cell[8 * chip + j] * face[8 * chip + j]
                        value = value - lower * reduced[-1]
                    reduced.append(value * gain[k, u, j])
                here = reduced[-1]
                spec[k, u, ROWS - 1, c] = here
                zsend[k, to, i, 2 + c] = here
                for j in range(ROWS - 2, -1, -1):
                    here = reduced[j] - ratio[k, u, j] * here
                    spec[k, u, j, c] = here
                zsend[k, to, i, c] = here

        for i in range(2):
            loop(0, CHIPS, lambda to: sweep(to, i))
            loop(1, CHIPS, lambda step: chip_copy(k, i, step).start())
            zrecv[k, chip, i] = zsend[k, chip, i]

    def chain_part(k, i):
        loop(1, CHIPS, lambda step: chip_in(k, i, step, zrecv, zr_sem).wait())
        for c in range(2):
            lead = zero
            ends, heads = [], []
            for block in range(CHIPS):
                y_low, y_high = zrecv[k, block, i, c], zrecv[k, block, i, 2 + c]
                end = y_low * chain[k, i, block, 2] + chain[k, i, block, 0] * lead
                lead = y_high + chain[k, i, block, 3] * (lead + chain[k, i, block, 4] * end)
                ends.append(end)
                heads.append(lead)
            from_high = zero
            for block in range(CHIPS - 1, -1, -1):
                zback[k, block, i, 2 + c] = from_high
                last = heads[block] + chain[k, i, block, 5] * from_high
                if block < CHIPS - 1:
                    zback[k, block + 1, i, c] = last
                from_high = ends[block] + chain[k, i, block, 1] * from_high
            zback[k, 0, i, c] = zero
        loop(1, CHIPS, lambda step: back_copy(k, i, step).start())
        zdone[k, chip, i] = zback[k, chip, i]

    my_rows = pl.ds(pl.multiple_of(16 * core, 16), 16)

    def place(u):
        return out.at[:, :, my_rows, pl.ds(pl.multiple_of(128 * u, 128), 128)]

    def swap_copy(u):
        return remote(
            stage.at[1 - core, u], place(u), swap_send.at[u], swap_recv.at[u], pln, wall + 1 - 2 * core
        )

    def keep_copy(u):
        return pltpu.make_async_copy(stage.at[core, u], place(u), end_sem.at[u])

    def result_part(k, i):
        loop(1, CHIPS, lambda step: chip_in(k, i, step, zdone, br_sem).wait())

        def finish(to):
            u = 2 * to + i
            for c in range(2):
                from_low, from_high = zdone[k, to, i, c], zdone[k, to, i, 2 + c]
                for j in range(ROWS):
                    value = spec[k, u, j, c] + low_end[k, u, j] * from_low + high_end[k, u, j] * from_high
                    stage[j // 4, u, c, j % 4, pl.ds(k, 8, stride=2), :] = value
            if k == 1:
                swap_copy(u).start()
                keep_copy(u).start()

        loop(0, CHIPS, finish)

    spectrum_part(0)
    chain_part(0, 0)
    chain_part(0, 1)
    spectrum_part(1)
    result_part(0, 0)
    result_part(0, 1)
    chain_part(1, 0)
    chain_part(1, 1)
    result_part(1, 0)
    result_part(1, 1)

    sent_part(1, 0)
    sent_part(1, 1)
    for k in range(2):
        for i in range(2):
            loop(1, CHIPS, lambda step: chip_copy(k, i, step).wait_send())
            loop(1, CHIPS, lambda step: back_copy(k, i, step).wait_send())
    loop(0, 16, lambda u: keep_copy(u).wait())
    loop(0, 16, lambda u: swap_copy(u).wait())


def per_device(vel_x, vel_y, vel_z, cell_metric, face_metric):
    anywhere = pl.BlockSpec(memory_space=pl.ANY)
    far = pl.BlockSpec(memory_space=pltpu.HBM)
    dma = pltpu.SemaphoreType.DMA
    return pl.pallas_call(
        kernel,
        out_shape=jax.ShapeDtypeStruct((2, 4, 32, NX), F32),
        in_specs=[far] * 10,
        out_specs=anywhere,
        scratch_shapes=[
            pltpu.SMEM((NY,), F32),
            pltpu.SMEM((NY + 1,), F32),
            pltpu.VMEM((4, 144, NZ), F32),
            pltpu.VMEM((6, 128, NZ), F32),
            pltpu.VMEM((4, 128, NZ), F32),
            pltpu.VMEM((2, 4, 1, NZ), F32),
            pltpu.VMEM((2, 4, 128, 512), BF16),
            pltpu.VMEM((2, 4, 128, 512), BF16),
            pltpu.VMEM((2, 2, 512, 512), BF16),
            pltpu.VMEM((2, 256, 256), BF16),
            pltpu.VMEM((16, 2, 8, 128), F32),
            pltpu.VMEM((16, 8, 128), F32),
            pltpu.VMEM((2, 8, 128), F32),
            pltpu.VMEM((2, 2, 512, 256), F32),
            pltpu.VMEM((2, 2, 2, PLN, 16, 256), F32),
            pltpu.VMEM((16, 64, 256), F32),
            pltpu.VMEM((16, 64, 256), F32),
            pltpu.VMEM((2, 16, ROWS, 2, 8, 128), F32),
            pltpu.VMEM((2, 16, ROWS, 8, 128), F32),
            pltpu.VMEM((2, 16, ROWS, 8, 128), F32),
            pltpu.VMEM((2, 16, ROWS, 8, 128), F32),
            pltpu.VMEM((2, 16, ROWS, 8, 128), F32),
            pltpu.VMEM((2, 2, CHIPS, 6, 8, 128), F32),
            pltpu.VMEM((2, CHIPS, 2, 4, 8, 128), F32),
            pltpu.VMEM((2, CHIPS, 2, 4, 8, 128), F32),
            pltpu.VMEM((2, CHIPS, 2, 4, 8, 128), F32),
            pltpu.VMEM((2, CHIPS, 2, 4, 8, 128), F32),
            pltpu.VMEM((2, 16, 2, 4, 16, 128), F32),
            dma((14,)),
            dma((4,)),
            dma((4,)),
            dma((2, 2)),
            dma((2, 2)),
            dma((2, 2, CHIPS)),
            dma((2, 2, CHIPS)),
            dma((2, 2, CHIPS)),
            dma((2, 2, CHIPS)),
            dma((16,)),
            dma((16,)),
            dma((16,)),
        ],
        compiler_params=pltpu.CompilerParams(
            collective_id=0, has_side_effects=True, vmem_limit_bytes=60 * 1024 * 1024
        ),
    )(vel_x, vel_y, vel_z, cell_metric, face_metric, *tables())


def solution(mesh):
    in_specs = (P("wall", "pln", None), P("wall", "pln", None), P("wall", "pln", None), P(), P())
    return jax.shard_map(
        per_device, mesh=mesh, in_specs=in_specs, out_specs=P(None, "wall", "pln", None), check_vma=False
    )
```

```python
import functools
import math

import jax
import jax.numpy as jnp
import numpy as np
from jax import lax
from jax.experimental import pallas as pl
from jax.experimental.pallas import tpu as pltpu
from jax.sharding import PartitionSpec as P
import ml_dtypes

MESH = pl.DeviceIdType.MESH
F32 = jnp.float32
BF16 = jnp.bfloat16
NX, NZ, NY = 2048, 1024, 64
PLN, CHIPS, ROWS = 16, 8, 8
PEERS = 2 * PLN
NT = (((1,), (1,)), ((), ()))
NN = (((1,), (0,)), ((), ()))


def halves(table):
    high = table.astype(ml_dtypes.bfloat16)
    low = (table - high.astype(np.float64)).astype(ml_dtypes.bfloat16)
    return np.stack([high, low])


@functools.lru_cache(None)
def tables():
    points = np.arange(512, dtype=np.float64)
    z_parts = []
    for parity in range(2):
        n = 2 * np.arange(256, dtype=np.int64) + parity
        phase = 2.0 * np.pi / NZ * ((n[:, None] * np.arange(512)[None, :]) % NZ)
        pair = np.stack([np.cos(phase), -np.sin(phase)]) / math.sqrt(NZ)
        rows = pair.reshape(2, PEERS, 8, 512).transpose(1, 0, 2, 3).reshape(512, 512)
        z_parts.append(halves(rows))
    z_table = np.stack(z_parts)
    lane = np.arange(128)
    s = 8 * (lane % 16) + lane // 16
    phase = 2.0 * np.pi / 128 * ((lane[:, None] * s[None, :]) % 128)
    cos, sin = -np.cos(phase) / math.sqrt(NX), -np.sin(phase) / math.sqrt(NX)
    x_table = halves(np.block([[cos, -sin], [sin, cos]]))
    turn = 2.0 * np.pi / NX * (np.arange(16)[:, None] * lane[None, :])
    twiddle = np.stack([np.cos(turn), -np.sin(turn)], axis=1).astype(np.float32)
    twiddle = np.broadcast_to(twiddle[:, :, None, :], (16, 2, 8, 128)).copy()
    m = np.arange(NX, dtype=np.float64)
    along_x = (2.0 - 2.0 * np.cos(2.0 * np.pi / NX * m)).astype(np.float32).reshape(16, 1, 128)
    along_x = np.broadcast_to(along_x, (16, 8, 128)).copy()
    n = np.arange(512, dtype=np.float64)
    along_z = (2.0 - 2.0 * np.cos(2.0 * np.pi / NZ * n)).astype(np.float32)
    along_z = along_z.reshape(PEERS, 8, 2).transpose(0, 2, 1)[..., None]
    along_z = np.broadcast_to(along_z, (PEERS, 2, 8, 128)).copy()
    return z_table, x_table, twiddle, along_x, along_z


def times(a, b):
    return a[0] * b[0] - a[1] * b[1], a[0] * b[1] + a[1] * b[0]


def add(a, b):
    return a[0] + b[0], a[1] + b[1]


def sub(a, b):
    return a[0] - b[0], a[1] - b[1]


def minus_i(a):
    return a[1], -a[0]


def four(a):
    s02, d02, s13, d13 = add(a[0], a[2]), sub(a[0], a[2]), add(a[1], a[3]), sub(a[1], a[3])
    d13 = minus_i(d13)
    return [add(s02, s13), add(d02, d13), sub(s02, s13), sub(d02, d13)]


def by_sixteenth(a, k):
    if k == 0:
        return a
    if k == 4:
        return minus_i(a)
    if k == 2:
        h = math.sqrt(0.5)
        return (a[0] + a[1]) * h, (a[1] - a[0]) * h
    if k == 6:
        h = math.sqrt(0.5)
        return (a[1] - a[0]) * h, (a[0] + a[1]) * (-h)
    angle = -2.0 * math.pi * k / 16
    c, s = math.cos(angle), math.sin(angle)
    return a[0] * c - a[1] * s, a[0] * s + a[1] * c


def sixteen(a):
    inner = [four([a[4 * p1 + p2] for p1 in range(4)]) for p2 in range(4)]
    out = [None] * 16
    for t1 in range(4):
        outer = four([by_sixteenth(inner[p2][t1], p2 * t1) for p2 in range(4)])
        for t2 in range(4):
            out[t1 + 4 * t2] = outer[t2]
    return out


def dot3(a_high, a_low, b_high, b_low, dims):
    dot = functools.partial(lax.dot_general, dimension_numbers=dims, preferred_element_type=F32)
    return dot(a_high, b_high) + (dot(a_low, b_high) + dot(a_high, b_low))


def split(value):
    high = value.astype(BF16)
    return high, (value - high.astype(F32)).astype(BF16)


def kernel(
    vel_x, vel_y, vel_z, cell_metric, face_metric, z_table, x_table, twiddle, along_x, along_z,
    out,
    cell, face, vx, vy, vz, edge_x, dhigh, dlow, ztab, xtab, twid, kx, kz,
    zout, recv, xin, xo, spec, gain, ratio, low_end, high_end,
    chain, zsend, zrecv, zback, zdone, stage,
    in_sem, halo_send, halo_recv, xs_sem, xr_sem, zs_sem, zr_sem, bs_sem, br_sem, end_sem, swap_send, swap_recv,
):
    pln, wall = lax.axis_index("pln"), lax.axis_index("wall")
    chip, core = lax.div(wall, 2), lax.rem(wall, 2)
    me = 2 * pln + core

    def x_rows(first, rows):
        return vel_x.at[pl.ds(first, rows)], vx.at[pl.ds(first, rows), pl.ds(8, 128), :]

    def z_rows(first, rows):
        return vel_z.at[pl.ds(first, rows)], vz.at[pl.ds(first, rows)]

    pairs = [
        (vel_y, vy.at[pl.ds(1, 4)]), x_rows(1, 2), z_rows(1, 2), (cell_metric, cell), (z_table, ztab),
        x_rows(0, 1), x_rows(3, 1), z_rows(0, 1), z_rows(3, 1), (face_metric, face),
        (x_table, xtab), (twiddle, twid), (along_x, kx), (along_z.at[me], kz),
    ]
    inputs = [pltpu.make_async_copy(src, dst, in_sem.at[at]) for at, (src, dst) in enumerate(pairs)]
    for copy in inputs:
        copy.start()

    barrier = pltpu.get_barrier_semaphore()

    def greet(pln_to, wall_to):
        pl.semaphore_signal(barrier, inc=1, device_id=(pln_to, wall_to), device_id_type=MESH)

    def peer(step):
        to = (me + step) & (PEERS - 1)
        return to, to >> 1, 2 * chip + (to & 1)

    def greet_peer(step, none):
        to, pln_to, wall_to = peer(step)
        greet(pln_to, wall_to)
        return none

    def greet_chip(step, none):
        greet(pln, 2 * lax.rem(chip + step, CHIPS) + core)
        return none

    lax.fori_loop(1, PEERS, greet_peer, 0)
    lax.fori_loop(1, CHIPS, greet_chip, 0)
    greet(pln, lax.rem(wall + 2 * core + 15, 16))
    pl.semaphore_wait(barrier, PEERS - 1 + CHIPS - 1 + 1)

    def remote(src, dst, send_sem, recv_sem, pln_to, wall_to):
        return pltpu.make_async_remote_copy(
            src_ref=src, dst_ref=dst, send_sem=send_sem, recv_sem=recv_sem,
            device_id=(pln_to, wall_to), device_id_type=MESH,
        )

    after, before = lax.rem(pln + 1, PLN), lax.rem(pln + PLN - 1, PLN)
    above, below = lax.rem(wall + 1, 16), lax.rem(wall + 15, 16)
    halos = [
        remote(vel_x.at[:, pl.ds(127, 1), :], edge_x.at[0], halo_send.at[0], halo_recv.at[0], after, wall),
        remote(vel_x.at[:, pl.ds(0, 1), :], edge_x.at[1], halo_send.at[1], halo_recv.at[1], before, wall),
        remote(vel_y.at[3], vy.at[0], halo_send.at[2], halo_recv.at[2], pln, above),
        remote(vel_y.at[0], vy.at[5], halo_send.at[3], halo_recv.at[3], pln, below),
    ]
    for copy in halos:
        copy.start()
    def diverge_row(j, slot, firsts):
        metric = cell[4 * wall + j] * 0.5
        from_low = jnp.where((wall == 0) & (j == 0), 0.0, metric)
        from_high = jnp.where((wall == 15) & (j == 3), 0.0, metric)
        for first in firsts:
            rows = slice(first, first + 32)
            along = vx[j, first + 9 : first + 41, :] - vx[j, first + 7 : first + 39, :]
            level = vz[j, rows, :]
            along = along + (pltpu.roll(level, NZ - 1, 1) - pltpu.roll(level, 1, 1))
            total = along * 0.5 + (vy[j + 2, rows, :] * from_high - vy[j, rows, :] * from_low)
            left, right = total[:, :512], total[:, 512:]
            dhigh[0, slot, rows, :], dlow[0, slot, rows, :] = split(left + right)
            dhigh[1, slot, rows, :], dlow[1, slot, rows, :] = split(left - right)

    def out_copy(k, part, step):
        to, pln_to, wall_to = peer(step)
        return remote(
            zout.at[k, part, pl.ds(pl.multiple_of(16 * to, 16), 16), :], recv.at[k, part, core, pln],
            xs_sem.at[k, part], xr_sem.at[k, part], pln_to, wall_to,
        )

    def arrived_part(k, part):
        pltpu.make_async_copy(recv.at[k, part], recv.at[k, part], xr_sem.at[k, part]).wait()

    def own_copy(k, part):
        return pltpu.make_async_copy(
            zout.at[k, part, pl.ds(pl.multiple_of(16 * me, 16), 16), :], recv.at[k, part, core, pln],
            xr_sem.at[k, part],
        )

    def loop(first, last, step):
        def body(at, none):
            step(at)
            return none

        lax.fori_loop(first, last, body, 0)

    def z_part(k, part):
        slots = slice(2 * part, 2 * part + 2)
        zout[k, part] = dot3(
            ztab[k, 0], ztab[k, 1], dhigh[k, slots].reshape(256, 512), dlow[k, slots].reshape(256, 512), NT
        )

    def send_part(k, part):
        loop(1, PEERS, lambda step: out_copy(k, part, step).start())
        own_copy(k, part).start()

    def sent_part(k, part):
        gone = zout.at[k, part, pl.ds(0, 16 * (PEERS - 1)), :]
        pltpu.make_async_copy(gone, gone, xs_sem.at[k, part]).wait()

    for copy in inputs[:4]:
        copy.wait()
    loop(0, 2, lambda i: diverge_row(1 + i, i, (32, 64)))
    halos[0].wait()
    halos[1].wait()
    for j in range(4):
        vx[j, 7:8, :] = edge_x[0, j]
        vx[j, 136:137, :] = edge_x[1, j]
    loop(0, 2, lambda i: diverge_row(1 + i, i, (0, 96)))
    inputs[4].wait()
    z_part(0, 0)
    send_part(0, 0)
    z_part(1, 0)
    for copy in inputs[5:10]:
        copy.wait()
    halos[2].wait()
    halos[3].wait()
    loop(0, 2, lambda i: diverge_row(3 * i, 2 + i, (0, 32, 64, 96)))
    z_part(0, 1)
    send_part(0, 1)
    z_part(1, 1)
    sent_part(0, 0)
    send_part(1, 0)
    for copy in inputs[10:]:
        copy.wait()

    def bands(row, square):
        metric, low, high = cell[row], face[row], face[row + 1]
        return -metric * low, -metric * high, metric * (low + high) + square

    def eliminate(first, square):
        gains, ratios, lowers, entered = [], [], [], []
        for j in range(ROWS):
            lower, upper, diag = bands(first + j, square)
            inverse = 1.0 / (diag if j == 0 else diag - lower * ratios[-1])
            gains.append(inverse)
            ratios.append(upper * inverse)
            entered.append((-lower) * inverse if j == 0 else (-lower) * entered[-1] * inverse)
            lowers.append(lower)
        return gains, ratios, entered

    def matrix_step(at, none):
        k, u = lax.div(at, 16), lax.rem(at, 16)
        gains, ratios, entered = eliminate(8 * chip, kx[u] + kz[k])
        from_low, from_high = entered[7], -ratios[7]
        for j in range(ROWS - 1, -1, -1):
            if j < ROWS - 1:
                from_low = entered[j] - ratios[j] * from_low
                from_high = -ratios[j] * from_high
            gain[k, u, j] = gains[j]
            ratio[k, u, j] = ratios[j]
            low_end[k, u, j] = from_low
            high_end[k, u, j] = from_high
        return none

    lax.fori_loop(0, 32, matrix_step, 0)

    def chain_step(block, held):
        heads = []
        for at in range(4):
            k, i = at // 2, at % 2
            gains, ratios, entered = eliminate(8 * block, kx[2 * chip + i] + kz[k])
            top_low, top_high = entered[7], -ratios[7]
            low, high = top_low, top_high
            for j in range(ROWS - 2, -1, -1):
                low, high = entered[j] - ratios[j] * low, -ratios[j] * high
            head = held[at]
            inverse = 1.0 / (1.0 - low * head)
            chain[k, i, block, 0] = low * inverse
            chain[k, i, block, 1] = high * inverse
            chain[k, i, block, 2] = inverse
            chain[k, i, block, 3] = top_low
            chain[k, i, block, 4] = head
            head = top_high + top_low * head * (high * inverse)
            chain[k, i, block, 5] = head
            heads.append(head)
        return tuple(heads)

    zero = jnp.zeros((8, 128), F32)
    lax.fori_loop(0, CHIPS, chain_step, (zero,) * 4)
    sent_part(0, 1)
    send_part(1, 1)

    lane = lax.broadcasted_iota(jnp.int32, (8, 128), 1)

    def chip_copy(k, i, step):
        to = (chip + step) & (CHIPS - 1)
        return remote(
            zsend.at[k, i, to], zrecv.at[k, i, chip], zs_sem.at[k, i], zr_sem.at[k, i], pln, 2 * to + core
        )

    def chip_wait(k, i, buffer, sems):
        blocks = buffer.at[k, i, pl.ds(0, CHIPS - 1)]
        pltpu.make_async_copy(blocks, blocks, sems.at[k, i]).wait()

    def back_copy(k, i, step):
        to = (chip + step) & (CHIPS - 1)
        return remote(
            zback.at[k, i, to], zdone.at[k, i, chip], bs_sem.at[k, i], br_sem.at[k, i], pln, 2 * to + core
        )

    def spectrum_part(k):
        def points(at, part):
            side, i = at >> 1, at & 1
            row = 4 * side + 1 + i - part + 2 * part * i
            lanes = pl.ds(pl.multiple_of(128 * i, 128), 128)
            rows = pl.ds(pl.multiple_of(8 * row, 8), 8)
            held = [
                (recv[k, part, side, p, 0:8, lanes], recv[k, part, side, p, 8:16, lanes]) for p in range(PLN)
            ]
            for t, value in enumerate(sixteen(held)):
                if t:
                    value = times(value, (twid[t, 0], twid[t, 1]))
                xin[t, rows, 0:128] = value[0]
                xin[t, rows, 128:256] = value[1]

        for part in range(2):
            arrived_part(k, part)
            loop(0, 4, lambda at: points(at, part))

        def product(group):
            some = pl.ds(4 * group, 4)
            high, low = split(xin[some].reshape(256, 256))
            xo[some] = dot3(high, low, xtab[0], xtab[1], NN).reshape(4, 64, 256)

        loop(0, 4, product)

        def order(row):
            rows = pl.ds(pl.multiple_of(8 * row, 8), 8)
            for c in range(2):
                held = [xo[t, rows, 128 * c : 128 * c + 128] for t in range(16)]
                held = [pltpu.roll(value, t, 1) if t else value for t, value in enumerate(held)]
                for bit in range(4):
                    chosen = (lane & (1 << bit)) != 0
                    held = [jnp.where(chosen, held[(t + (1 << bit)) % 16], held[t]) for t in range(16)]
                for u in range(16):
                    value = held[(16 - u) % 16]
                    spec[k, u, row, c] = pltpu.roll(value, 128 - u, 1) if u else value

        loop(0, ROWS, order)

        def sweep(to, i):
            u = 2 * to + i
            for c in range(2):
                reduced = []
                for j in range(ROWS):
                    value = spec[k, u, j, c]
                    if j:
                        lower = -cell[8 * chip + j] * face[8 * chip + j]
                        value = value - lower * reduced[-1]
                    reduced.append(value * gain[k, u, j])
                here = reduced[-1]
                spec[k, u, ROWS - 1, c] = here
                zsend[k, i, to, 2 + c] = here
                for j in range(ROWS - 2, -1, -1):
                    here = reduced[j] - ratio[k, u, j] * here
                    spec[k, u, j, c] = here
                zsend[k, i, to, c] = here

        for i in range(2):
            loop(0, CHIPS, lambda to: sweep(to, i))
            loop(1, CHIPS, lambda step: chip_copy(k, i, step).start())
            zrecv[k, i, chip] = zsend[k, i, chip]

    def chain_part(k, i):
        chip_wait(k, i, zrecv, zr_sem)
        for c in range(2):
            lead = zero
            ends, heads = [], []
            for block in range(CHIPS):
                y_low, y_high = zrecv[k, i, block, c], zrecv[k, i, block, 2 + c]
                end = y_low * chain[k, i, block, 2] + chain[k, i, block, 0] * lead
                lead = y_high + chain[k, i, block, 3] * (lead + chain[k, i, block, 4] * end)
                ends.append(end)
                heads.append(lead)
            from_high = zero
            for block in range(CHIPS - 1, -1, -1):
                zback[k, i, block, 2 + c] = from_high
                last = heads[block] + chain[k, i, block, 5] * from_high
                if block < CHIPS - 1:
                    zback[k, i, block + 1, c] = last
                from_high = ends[block] + chain[k, i, block, 1] * from_high
            zback[k, i, 0, c] = zero
        loop(1, CHIPS, lambda step: back_copy(k, i, step).start())
        zdone[k, i, chip] = zback[k, i, chip]

    my_rows = pl.ds(pl.multiple_of(16 * core, 16), 16)

    def place(u):
        return out.at[:, :, my_rows, pl.ds(pl.multiple_of(128 * u, 128), 128)]

    def swap_copy(u):
        return remote(
            stage.at[1 - core, u], place(u), swap_send.at[0], swap_recv.at[0], pln, wall + 1 - 2 * core
        )

    def keep_copy(u):
        return pltpu.make_async_copy(stage.at[core, u], place(u), end_sem.at[0])

    def result_part(k, i):
        chip_wait(k, i, zdone, br_sem)

        def finish(to):
            u = 2 * to + i
            for c in range(2):
                from_low, from_high = zdone[k, i, to, c], zdone[k, i, to, 2 + c]
                for j in range(ROWS):
                    value = spec[k, u, j, c] + low_end[k, u, j] * from_low + high_end[k, u, j] * from_high
                    stage[j // 4, u, c, j % 4, pl.ds(k, 8, stride=2), :] = value
            if k == 1:
                swap_copy(u).start()
                keep_copy(u).start()

        loop(0, CHIPS, finish)

    spectrum_part(0)
    chain_part(0, 0)
    chain_part(0, 1)
    spectrum_part(1)
    result_part(0, 0)
    result_part(0, 1)
    chain_part(1, 0)
    chain_part(1, 1)
    result_part(1, 0)
    result_part(1, 1)

    sent_part(1, 0)
    sent_part(1, 1)
    for k in range(2):
        for i in range(2):
            chip_wait(k, i, zsend, zs_sem)
            chip_wait(k, i, zback, bs_sem)
    for side, sem in ((core, end_sem), (1 - core, swap_send), (1 - core, swap_recv)):
        pltpu.make_async_copy(stage.at[side], stage.at[side], sem.at[0]).wait()


def per_device(vel_x, vel_y, vel_z, cell_metric, face_metric):
    anywhere = pl.BlockSpec(memory_space=pl.ANY)
    far = pl.BlockSpec(memory_space=pltpu.HBM)
    dma = pltpu.SemaphoreType.DMA
    return pl.pallas_call(
        kernel,
        out_shape=jax.ShapeDtypeStruct((2, 4, 32, NX), F32),
        in_specs=[far] * 10,
        out_specs=anywhere,
        scratch_shapes=[
            pltpu.SMEM((NY,), F32),
            pltpu.SMEM((NY + 1,), F32),
            pltpu.VMEM((4, 144, NZ), F32),
            pltpu.VMEM((6, 128, NZ), F32),
            pltpu.VMEM((4, 128, NZ), F32),
            pltpu.VMEM((2, 4, 1, NZ), F32),
            pltpu.VMEM((2, 4, 128, 512), BF16),
            pltpu.VMEM((2, 4, 128, 512), BF16),
            pltpu.VMEM((2, 2, 512, 512), BF16),
            pltpu.VMEM((2, 256, 256), BF16),
            pltpu.VMEM((16, 2, 8, 128), F32),
            pltpu.VMEM((16, 8, 128), F32),
            pltpu.VMEM((2, 8, 128), F32),
            pltpu.VMEM((2, 2, 512, 256), F32),
            pltpu.VMEM((2, 2, 2, PLN, 16, 256), F32),
            pltpu.VMEM((16, 64, 256), F32),
            pltpu.VMEM((16, 64, 256), F32),
            pltpu.VMEM((2, 16, ROWS, 2, 8, 128), F32),
            pltpu.VMEM((2, 16, ROWS, 8, 128), F32),
            pltpu.VMEM((2, 16, ROWS, 8, 128), F32),
            pltpu.VMEM((2, 16, ROWS, 8, 128), F32),
            pltpu.VMEM((2, 16, ROWS, 8, 128), F32),
            pltpu.VMEM((2, 2, CHIPS, 6, 8, 128), F32),
            pltpu.VMEM((2, 2, CHIPS, 4, 8, 128), F32),
            pltpu.VMEM((2, 2, CHIPS, 4, 8, 128), F32),
            pltpu.VMEM((2, 2, CHIPS, 4, 8, 128), F32),
            pltpu.VMEM((2, 2, CHIPS, 4, 8, 128), F32),
            pltpu.VMEM((2, 16, 2, 4, 16, 128), F32),
            dma((14,)),
            dma((4,)),
            dma((4,)),
            dma((2, 2)),
            dma((2, 2)),
            dma((2, 2)),
            dma((2, 2)),
            dma((2, 2)),
            dma((2, 2)),
            dma((1,)),
            dma((1,)),
            dma((1,)),
        ],
        compiler_params=pltpu.CompilerParams(
            collective_id=0, has_side_effects=True, vmem_limit_bytes=60 * 1024 * 1024
        ),
    )(vel_x, vel_y, vel_z, cell_metric, face_metric, *tables())


def solution(mesh):
    in_specs = (P("wall", "pln", None), P("wall", "pln", None), P("wall", "pln", None), P(), P())
    return jax.shard_map(
        per_device, mesh=mesh, in_specs=in_specs, out_specs=P(None, "wall", "pln", None), check_vma=False
    )
```

```python
import functools
import math

import jax
import jax.numpy as jnp
import numpy as np
from jax import lax
from jax.experimental import pallas as pl
from jax.experimental.pallas import tpu as pltpu
from jax.sharding import PartitionSpec as P
import ml_dtypes

MESH = pl.DeviceIdType.MESH
F32 = jnp.float32
BF16 = jnp.bfloat16
NX, NZ, NY = 2048, 1024, 64
PLN, CHIPS, ROWS = 16, 8, 8
PEERS = 2 * PLN
NT = (((1,), (1,)), ((), ()))
NN = (((1,), (0,)), ((), ()))


def halves(table):
    high = table.astype(ml_dtypes.bfloat16)
    low = (table - high.astype(np.float64)).astype(ml_dtypes.bfloat16)
    return np.stack([high, low])


@functools.lru_cache(None)
def tables():
    points = np.arange(512, dtype=np.float64)
    z_parts = []
    for parity in range(2):
        n = 2 * np.arange(256, dtype=np.int64) + parity
        phase = 2.0 * np.pi / NZ * ((n[:, None] * np.arange(512)[None, :]) % NZ)
        pair = np.stack([np.cos(phase), -np.sin(phase)]) / math.sqrt(NZ)
        rows = pair.reshape(2, PEERS, 8, 512).transpose(1, 0, 2, 3).reshape(512, 512)
        z_parts.append(halves(rows))
    z_table = np.stack(z_parts)
    lane = np.arange(128)
    s = 8 * (lane % 16) + lane // 16
    phase = 2.0 * np.pi / 128 * ((lane[:, None] * s[None, :]) % 128)
    cos, sin = -np.cos(phase) / math.sqrt(NX), -np.sin(phase) / math.sqrt(NX)
    x_table = halves(np.block([[cos, -sin], [sin, cos]]))
    turn = 2.0 * np.pi / NX * (np.arange(16)[:, None] * lane[None, :])
    twiddle = np.stack([np.cos(turn), -np.sin(turn)], axis=1).astype(np.float32)
    twiddle = np.broadcast_to(twiddle[:, :, None, :], (16, 2, 8, 128)).copy()
    m = np.arange(NX, dtype=np.float64)
    along_x = (2.0 - 2.0 * np.cos(2.0 * np.pi / NX * m)).astype(np.float32).reshape(16, 1, 128)
    along_x = np.broadcast_to(along_x, (16, 8, 128)).copy()
    n = np.arange(512, dtype=np.float64)
    along_z = (2.0 - 2.0 * np.cos(2.0 * np.pi / NZ * n)).astype(np.float32)
    along_z = along_z.reshape(PEERS, 8, 2).transpose(0, 2, 1)[..., None]
    along_z = np.broadcast_to(along_z, (PEERS, 2, 8, 128)).copy()
    return z_table, x_table, twiddle, along_x, along_z


def times(a, b):
    return a[0] * b[0] - a[1] * b[1], a[0] * b[1] + a[1] * b[0]


def add(a, b):
    return a[0] + b[0], a[1] + b[1]


def sub(a, b):
    return a[0] - b[0], a[1] - b[1]


def minus_i(a):
    return a[1], -a[0]


def four(a):
    s02, d02, s13, d13 = add(a[0], a[2]), sub(a[0], a[2]), add(a[1], a[3]), sub(a[1], a[3])
    d13 = minus_i(d13)
    return [add(s02, s13), add(d02, d13), sub(s02, s13), sub(d02, d13)]


def by_sixteenth(a, k):
    if k == 0:
        return a
    if k == 4:
        return minus_i(a)
    if k == 2:
        h = math.sqrt(0.5)
        return (a[0] + a[1]) * h, (a[1] - a[0]) * h
    if k == 6:
        h = math.sqrt(0.5)
        return (a[1] - a[0]) * h, (a[0] + a[1]) * (-h)
    angle = -2.0 * math.pi * k / 16
    c, s = math.cos(angle), math.sin(angle)
    return a[0] * c - a[1] * s, a[0] * s + a[1] * c


def sixteen(a):
    inner = [four([a[4 * p1 + p2] for p1 in range(4)]) for p2 in range(4)]
    out = [None] * 16
    for t1 in range(4):
        outer = four([by_sixteenth(inner[p2][t1], p2 * t1) for p2 in range(4)])
        for t2 in range(4):
            out[t1 + 4 * t2] = outer[t2]
    return out


def dot3(a_high, a_low, b_high, b_low, dims):
    dot = functools.partial(lax.dot_general, dimension_numbers=dims, preferred_element_type=F32)
    return dot(a_high, b_high) + (dot(a_low, b_high) + dot(a_high, b_low))


def split(value):
    high = value.astype(BF16)
    return high, (value - high.astype(F32)).astype(BF16)


def kernel(
    vel_x, vel_y, vel_z, cell_metric, face_metric, z_table, x_table, twiddle, along_x, along_z,
    out,
    cell, face, vx, vy, vz, edge_x, dhigh, dlow, ztab, xtab, twid, kx, kz,
    zout, recv, xin, xo, spec, gain, ratio, low_end, high_end,
    chain, zsend, zrecv, zback, zdone, stage,
    in_sem, halo_send, halo_recv, xs_sem, xr_sem, zs_sem, zr_sem, bs_sem, br_sem, end_sem, swap_send, swap_recv,
):
    pln, wall = lax.axis_index("pln"), lax.axis_index("wall")
    chip, core = lax.div(wall, 2), lax.rem(wall, 2)
    me = 2 * pln + core

    def x_rows(first, rows):
        return vel_x.at[pl.ds(first, rows)], vx.at[pl.ds(first, rows), pl.ds(8, 128), :]

    def z_rows(first, rows):
        return vel_z.at[pl.ds(first, rows)], vz.at[pl.ds(first, rows)]

    pairs = [
        (vel_y, vy.at[pl.ds(1, 4)]), x_rows(1, 2), z_rows(1, 2), (cell_metric, cell), (z_table, ztab),
        x_rows(0, 1), x_rows(3, 1), z_rows(0, 1), z_rows(3, 1), (face_metric, face),
        (x_table, xtab), (twiddle, twid), (along_x, kx), (along_z.at[me], kz),
    ]
    inputs = [pltpu.make_async_copy(src, dst, in_sem.at[at]) for at, (src, dst) in enumerate(pairs)]
    for copy in inputs:
        copy.start()

    barrier = pltpu.get_barrier_semaphore()

    def greet(pln_to, wall_to):
        pl.semaphore_signal(barrier, inc=1, device_id=(pln_to, wall_to), device_id_type=MESH)

    def peer(step):
        to = (me + step) & (PEERS - 1)
        return to, to >> 1, 2 * chip + (to & 1)

    def greet_peer(step, none):
        to, pln_to, wall_to = peer(step)
        greet(pln_to, wall_to)
        return none

    def greet_chip(step, none):
        greet(pln, 2 * lax.rem(chip + step, CHIPS) + core)
        return none

    lax.fori_loop(1, PEERS, greet_peer, 0)
    lax.fori_loop(1, CHIPS, greet_chip, 0)
    greet(pln, lax.rem(wall + 2 * core + 15, 16))
    pl.semaphore_wait(barrier, PEERS - 1 + CHIPS - 1 + 1)

    def remote(src, dst, send_sem, recv_sem, pln_to, wall_to):
        return pltpu.make_async_remote_copy(
            src_ref=src, dst_ref=dst, send_sem=send_sem, recv_sem=recv_sem,
            device_id=(pln_to, wall_to), device_id_type=MESH,
        )

    after, before = lax.rem(pln + 1, PLN), lax.rem(pln + PLN - 1, PLN)
    above, below = lax.rem(wall + 1, 16), lax.rem(wall + 15, 16)
    halos = [
        remote(vel_x.at[:, pl.ds(127, 1), :], edge_x.at[0], halo_send.at[0], halo_recv.at[0], after, wall),
        remote(vel_x.at[:, pl.ds(0, 1), :], edge_x.at[1], halo_send.at[1], halo_recv.at[1], before, wall),
        remote(vel_y.at[3], vy.at[0], halo_send.at[2], halo_recv.at[2], pln, above),
        remote(vel_y.at[0], vy.at[5], halo_send.at[3], halo_recv.at[3], pln, below),
    ]
    for copy in halos:
        copy.start()
    def diverge_row(j, slot, firsts):
        metric = cell[4 * wall + j] * 0.5
        from_low = jnp.where((wall == 0) & (j == 0), 0.0, metric)
        from_high = jnp.where((wall == 15) & (j == 3), 0.0, metric)
        for first in firsts:
            rows = slice(first, first + 32)
            along = vx[j, first + 9 : first + 41, :] - vx[j, first + 7 : first + 39, :]
            level = vz[j, rows, :]
            along = along + (pltpu.roll(level, NZ - 1, 1) - pltpu.roll(level, 1, 1))
            total = along * 0.5 + (vy[j + 2, rows, :] * from_high - vy[j, rows, :] * from_low)
            left, right = total[:, :512], total[:, 512:]
            dhigh[0, slot, rows, :], dlow[0, slot, rows, :] = split(left + right)
            dhigh[1, slot, rows, :], dlow[1, slot, rows, :] = split(left - right)

    def out_copy(k, part, step):
        to, pln_to, wall_to = peer(step)
        return remote(
            zout.at[k, part, pl.ds(pl.multiple_of(16 * to, 16), 16), :], recv.at[k, part, core, pln],
            xs_sem.at[k, part], xr_sem.at[k, part], pln_to, wall_to,
        )

    def arrived_part(k, part):
        pltpu.make_async_copy(recv.at[k, part], recv.at[k, part], xr_sem.at[k, part]).wait()

    def own_copy(k, part):
        return pltpu.make_async_copy(
            zout.at[k, part, pl.ds(pl.multiple_of(16 * me, 16), 16), :], recv.at[k, part, core, pln],
            xr_sem.at[k, part],
        )

    def loop(first, last, step):
        def body(at, none):
            step(at)
            return none

        lax.fori_loop(first, last, body, 0)

    def z_part(k, part):
        slots = slice(2 * part, 2 * part + 2)
        zout[k, part] = dot3(
            ztab[k, 0], ztab[k, 1], dhigh[k, slots].reshape(256, 512), dlow[k, slots].reshape(256, 512), NT
        )

    def send_part(k, part):
        loop(1, PEERS, lambda step: out_copy(k, part, step).start())
        own_copy(k, part).start()

    def sent_part(k, part):
        gone = zout.at[k, part, pl.ds(0, 16 * (PEERS - 1)), :]
        pltpu.make_async_copy(gone, gone, xs_sem.at[k, part]).wait()

    for copy in inputs[:4]:
        copy.wait()
    loop(0, 2, lambda i: diverge_row(1 + i, i, (32, 64)))
    halos[0].wait()
    halos[1].wait()
    for j in range(4):
        vx[j, 7:8, :] = edge_x[0, j]
        vx[j, 136:137, :] = edge_x[1, j]
    loop(0, 2, lambda i: diverge_row(1 + i, i, (0, 96)))
    inputs[4].wait()
    z_part(0, 0)
    send_part(0, 0)
    z_part(1, 0)
    for copy in inputs[5:10]:
        copy.wait()
    halos[2].wait()
    halos[3].wait()
    loop(0, 2, lambda i: diverge_row(3 * i, 2 + i, (0, 32, 64, 96)))
    z_part(0, 1)
    send_part(0, 1)
    z_part(1, 1)
    sent_part(0, 0)
    send_part(1, 0)
    for copy in inputs[10:]:
        copy.wait()

    def bands(row, square):
        metric, low, high = cell[row], face[row], face[row + 1]
        return -metric * low, -metric * high, metric * (low + high) + square

    def eliminate(first, square):
        gains, ratios, lowers, entered = [], [], [], []
        for j in range(ROWS):
            lower, upper, diag = bands(first + j, square)
            inverse = 1.0 / (diag if j == 0 else diag - lower * ratios[-1])
            gains.append(inverse)
            ratios.append(upper * inverse)
            entered.append((-lower) * inverse if j == 0 else (-lower) * entered[-1] * inverse)
            lowers.append(lower)
        return gains, ratios, entered

    def matrix_step(at, none):
        k, u = lax.div(at, 16), lax.rem(at, 16)
        gains, ratios, entered = eliminate(8 * chip, kx[u] + kz[k])
        from_low, from_high = entered[7], -ratios[7]
        for j in range(ROWS - 1, -1, -1):
            if j < ROWS - 1:
                from_low = entered[j] - ratios[j] * from_low
                from_high = -ratios[j] * from_high
            gain[k, u, j] = gains[j]
            ratio[k, u, j] = ratios[j]
            low_end[k, u, j] = from_low
            high_end[k, u, j] = from_high
        return none

    lax.fori_loop(0, 32, matrix_step, 0)

    def chain_step(block, held):
        heads = []
        for at in range(4):
            k, i = at // 2, at % 2
            gains, ratios, entered = eliminate(8 * block, kx[2 * chip + i] + kz[k])
            top_low, top_high = entered[7], -ratios[7]
            low, high = top_low, top_high
            for j in range(ROWS - 2, -1, -1):
                low, high = entered[j] - ratios[j] * low, -ratios[j] * high
            head = held[at]
            inverse = 1.0 / (1.0 - low * head)
            chain[k, i, block, 0] = low * inverse
            chain[k, i, block, 1] = high * inverse
            chain[k, i, block, 2] = inverse
            chain[k, i, block, 3] = top_low
            chain[k, i, block, 4] = head
            head = top_high + top_low * head * (high * inverse)
            chain[k, i, block, 5] = head
            heads.append(head)
        return tuple(heads)

    zero = jnp.zeros((8, 128), F32)
    lax.fori_loop(0, CHIPS, chain_step, (zero,) * 4)
    sent_part(0, 1)
    send_part(1, 1)

    lane = lax.broadcasted_iota(jnp.int32, (8, 128), 1)

    def chip_copy(k, i, step):
        to = (chip + step) & (CHIPS - 1)
        return remote(
            zsend.at[k, i, to], zrecv.at[k, i, chip], zs_sem.at[k, i], zr_sem.at[k, i], pln, 2 * to + core
        )

    def chip_wait(k, i, buffer, sems):
        blocks = buffer.at[k, i, pl.ds(0, CHIPS - 1)]
        pltpu.make_async_copy(blocks, blocks, sems.at[k, i]).wait()

    def back_copy(k, i, step):
        to = (chip + step) & (CHIPS - 1)
        return remote(
            zback.at[k, i, to], zdone.at[k, i, chip], bs_sem.at[k, i], br_sem.at[k, i], pln, 2 * to + core
        )

    def spectrum_part(k):
        def points(at, part):
            side, i = at >> 1, at & 1
            row = 4 * side + 1 + i - part + 2 * part * i
            lanes = pl.ds(pl.multiple_of(128 * i, 128), 128)
            rows = pl.ds(pl.multiple_of(8 * row, 8), 8)
            held = [
                (recv[k, part, side, p, 0:8, lanes], recv[k, part, side, p, 8:16, lanes]) for p in range(PLN)
            ]
            for t, value in enumerate(sixteen(held)):
                if t:
                    value = times(value, (twid[t, 0], twid[t, 1]))
                xin[t, rows, 0:128] = value[0]
                xin[t, rows, 128:256] = value[1]

        for part in range(2):
            arrived_part(k, part)
            loop(0, 4, lambda at: points(at, part))

        def product(group):
            some = pl.ds(4 * group, 4)
            high, low = split(xin[some].reshape(256, 256))
            xo[some] = dot3(high, low, xtab[0], xtab[1], NN).reshape(4, 64, 256)

        for group in range(4):
            product(group)

        def order(row):
            rows = pl.ds(pl.multiple_of(8 * row, 8), 8)
            for c in range(2):
                held = [xo[t, rows, 128 * c : 128 * c + 128] for t in range(16)]
                held = [pltpu.roll(value, t, 1) if t else value for t, value in enumerate(held)]
                for bit in range(4):
                    chosen = (lane & (1 << bit)) != 0
                    held = [jnp.where(chosen, held[(t + (1 << bit)) % 16], held[t]) for t in range(16)]
                for u in range(16):
                    value = held[(16 - u) % 16]
                    spec[k, u, row, c] = pltpu.roll(value, 128 - u, 1) if u else value

        loop(0, ROWS, order)

        def sweep(group, i):
            tos = [2 * group + d for d in range(2)]
            lines = [(d, c) for d in range(len(tos)) for c in range(2)]
            lowers = [-cell[8 * chip + j] * face[8 * chip + j] for j in range(ROWS)]
            gains = [[gain[k, 2 * to + i, j] for j in range(ROWS)] for to in tos]
            ratios = [[ratio[k, 2 * to + i, j] for j in range(ROWS)] for to in tos]
            held = [[spec[k, 2 * tos[d] + i, j, c] for j in range(ROWS)] for d, c in lines]
            for j in range(ROWS):
                for at, (d, c) in enumerate(lines):
                    value = held[at][j]
                    if j:
                        value = value - lowers[j] * held[at][j - 1]
                    held[at][j] = value * gains[d][j]
            for j in range(ROWS - 2, -1, -1):
                for at, (d, c) in enumerate(lines):
                    held[at][j] = held[at][j] - ratios[d][j] * held[at][j + 1]
            for at, (d, c) in enumerate(lines):
                for j in range(ROWS):
                    spec[k, 2 * tos[d] + i, j, c] = held[at][j]
                zsend[k, i, tos[d], 2 + c] = held[at][ROWS - 1]
                zsend[k, i, tos[d], c] = held[at][0]

        for i in range(2):
            loop(0, CHIPS // 2, lambda group: sweep(group, i))
            loop(1, CHIPS, lambda step: chip_copy(k, i, step).start())
            zrecv[k, i, chip] = zsend[k, i, chip]

    def chain_part(k, i):
        chip_wait(k, i, zrecv, zr_sem)
        for c in range(2):
            lead = zero
            ends, heads = [], []
            for block in range(CHIPS):
                y_low, y_high = zrecv[k, i, block, c], zrecv[k, i, block, 2 + c]
                end = y_low * chain[k, i, block, 2] + chain[k, i, block, 0] * lead
                lead = y_high + chain[k, i, block, 3] * (lead + chain[k, i, block, 4] * end)
                ends.append(end)
                heads.append(lead)
            from_high = zero
            for block in range(CHIPS - 1, -1, -1):
                zback[k, i, block, 2 + c] = from_high
                last = heads[block] + chain[k, i, block, 5] * from_high
                if block < CHIPS - 1:
                    zback[k, i, block + 1, c] = last
                from_high = ends[block] + chain[k, i, block, 1] * from_high
            zback[k, i, 0, c] = zero
        loop(1, CHIPS, lambda step: back_copy(k, i, step).start())
        zdone[k, i, chip] = zback[k, i, chip]

    my_rows = pl.ds(pl.multiple_of(16 * core, 16), 16)

    def place(u):
        return out.at[:, :, my_rows, pl.ds(pl.multiple_of(128 * u, 128), 128)]

    def swap_copy(u):
        return remote(
            stage.at[1 - core, u], place(u), swap_send.at[0], swap_recv.at[0], pln, wall + 1 - 2 * core
        )

    def keep_copy(u):
        return pltpu.make_async_copy(stage.at[core, u], place(u), end_sem.at[0])

    def result_part(k, i):
        chip_wait(k, i, zdone, br_sem)

        def finish(to):
            u = 2 * to + i
            for c in range(2):
                from_low, from_high = zdone[k, i, to, c], zdone[k, i, to, 2 + c]
                for j in range(ROWS):
                    value = spec[k, u, j, c] + low_end[k, u, j] * from_low + high_end[k, u, j] * from_high
                    stage[j // 4, u, c, j % 4, pl.ds(k, 8, stride=2), :] = value
            if k == 1:
                swap_copy(u).start()
                keep_copy(u).start()

        loop(0, CHIPS, finish)

    spectrum_part(0)
    chain_part(0, 0)
    chain_part(0, 1)
    spectrum_part(1)
    result_part(0, 0)
    result_part(0, 1)
    chain_part(1, 0)
    chain_part(1, 1)
    result_part(1, 0)
    result_part(1, 1)

    sent_part(1, 0)
    sent_part(1, 1)
    for k in range(2):
        for i in range(2):
            chip_wait(k, i, zsend, zs_sem)
            chip_wait(k, i, zback, bs_sem)
    for side, sem in ((core, end_sem), (1 - core, swap_send), (1 - core, swap_recv)):
        pltpu.make_async_copy(stage.at[side], stage.at[side], sem.at[0]).wait()


def per_device(vel_x, vel_y, vel_z, cell_metric, face_metric):
    anywhere = pl.BlockSpec(memory_space=pl.ANY)
    far = pl.BlockSpec(memory_space=pltpu.HBM)
    dma = pltpu.SemaphoreType.DMA
    return pl.pallas_call(
        kernel,
        out_shape=jax.ShapeDtypeStruct((2, 4, 32, NX), F32),
        in_specs=[far] * 10,
        out_specs=anywhere,
        scratch_shapes=[
            pltpu.SMEM((NY,), F32),
            pltpu.SMEM((NY + 1,), F32),
            pltpu.VMEM((4, 144, NZ), F32),
            pltpu.VMEM((6, 128, NZ), F32),
            pltpu.VMEM((4, 128, NZ), F32),
            pltpu.VMEM((2, 4, 1, NZ), F32),
            pltpu.VMEM((2, 4, 128, 512), BF16),
            pltpu.VMEM((2, 4, 128, 512), BF16),
            pltpu.VMEM((2, 2, 512, 512), BF16),
            pltpu.VMEM((2, 256, 256), BF16),
            pltpu.VMEM((16, 2, 8, 128), F32),
            pltpu.VMEM((16, 8, 128), F32),
            pltpu.VMEM((2, 8, 128), F32),
            pltpu.VMEM((2, 2, 512, 256), F32),
            pltpu.VMEM((2, 2, 2, PLN, 16, 256), F32),
            pltpu.VMEM((16, 64, 256), F32),
            pltpu.VMEM((16, 64, 256), F32),
            pltpu.VMEM((2, 16, ROWS, 2, 8, 128), F32),
            pltpu.VMEM((2, 16, ROWS, 8, 128), F32),
            pltpu.VMEM((2, 16, ROWS, 8, 128), F32),
            pltpu.VMEM((2, 16, ROWS, 8, 128), F32),
            pltpu.VMEM((2, 16, ROWS, 8, 128), F32),
            pltpu.VMEM((2, 2, CHIPS, 6, 8, 128), F32),
            pltpu.VMEM((2, 2, CHIPS, 4, 8, 128), F32),
            pltpu.VMEM((2, 2, CHIPS, 4, 8, 128), F32),
            pltpu.VMEM((2, 2, CHIPS, 4, 8, 128), F32),
            pltpu.VMEM((2, 2, CHIPS, 4, 8, 128), F32),
            pltpu.VMEM((2, 16, 2, 4, 16, 128), F32),
            dma((14,)),
            dma((4,)),
            dma((4,)),
            dma((2, 2)),
            dma((2, 2)),
            dma((2, 2)),
            dma((2, 2)),
            dma((2, 2)),
            dma((2, 2)),
            dma((1,)),
            dma((1,)),
            dma((1,)),
        ],
        compiler_params=pltpu.CompilerParams(
            collective_id=0, has_side_effects=True, vmem_limit_bytes=60 * 1024 * 1024
        ),
    )(vel_x, vel_y, vel_z, cell_metric, face_metric, *tables())


def solution(mesh):
    in_specs = (P("wall", "pln", None), P("wall", "pln", None), P("wall", "pln", None), P(), P())
    return jax.shard_map(
        per_device, mesh=mesh, in_specs=in_specs, out_specs=P(None, "wall", "pln", None), check_vma=False
    )
```
